256 devices in a mesh: dom: 16 (over y, x), panel: 16 (over z, core).
Axes of the slice: x: 4, y: 4, z: 8, core: 2. Of those that a mesh axis runs over, the one named last changes fastest.
Arguments:
- start_block: float32 [256, 16384], P('panel', 'dom'), may hold values from -1500 to 1500
- prior_dirs: float32 [256, 16384], P('panel', 'dom'), may hold values from -6 to 6
- degree: float32 [16384], P('dom'), may hold values from 1 to 4
- tiles: float32 [512, 128, 128], P('dom'), may hold values from -0.21875 to 0.21875
- tile_rows: int32 [512], P('dom'), may hold values from 0 to 7
- tile_cols: int32 [512], P('dom'), may hold values from 0 to 7
- cut_rows: int32 [4096], P('dom'), may hold values from 0 to 1023
- cut_count: int32 [16], P('dom'), may hold values from 128 to 256, as said below
- bound_tiles: float32 [256, 128, 128], P('dom'), may hold values from -0.21875 to 0.21875
- bound_rows: int32 [256], P('dom'), may hold values from 0 to 7
- bound_cols: int32 [256], P('dom'), may hold values from 0 to 31
- rot_xx: float32 [256, 256], replicated, may hold values from -0.21875 to 0.21875
- rot_xr: float32 [256, 256], replicated, may hold values from -0.21875 to 0.21875
- rot_xp: float32 [256, 256], replicated, may hold values from -0.21875 to 0.21875
- rot_pr: float32 [256, 256], replicated, may hold values from -0.25 to 0.25
- rot_pp: float32 [256, 256], replicated, may hold values from -0.25 to 0.25
Outputs:
- block: float32 [256, 16384], P('panel', 'dom')
- directions: float32 [256, 16384], P('panel', 'dom')
- ritz: float32 [256], P('panel')
The draws below stay inside these ranges and needn't reach their ends.
Inputs may be any that keep to these rules, and one draw needn't show every extreme that they name: `cut_count`: at most 256 live entries in a group's cut list; in every draw some group has exactly 256.
All inputs are finite; a program needn't handle non-finite values.
Results may differ from the reference program's by a relative error of at most 0.0003.
Values sent between devices are 32-bit elements; how exact they have to be, the bound alone decides.
A program may use at most 64 MiB of HBM per device.

```python
import math
import jax
import jax.numpy as jnp
from jax import lax

M = 256
TILE = 128
NDEV = 1024
BCUT = 256
TPR = 4
CTR = 2
ITERS = 4
TILES = 32
CT = 16
NODES = 16384
N_DOM = 16


def draw_start_block(key, part):
    key = jax.random.fold_in(key, 11)
    first, second, third = jax.random.split(key, 3)
    node = jnp.arange(NODES, dtype=jnp.float32)
    trend = jnp.power(3.0, node / NODES)
    row_scale = jnp.exp(jax.random.uniform(second, (NODES,), jnp.float32) * jnp.log(10.0))
    col_scale = jnp.exp(jax.random.uniform(third, (M, 1), jnp.float32) * jnp.log(10.0))
    base = jnp.clip(jax.random.normal(first, (M, NODES), jnp.float32), -5.0, 5.0)
    return base * row_scale[None, :] * col_scale * trend[None, :]


def draw_cut_count(key, part):
    key = jax.random.fold_in(key, 23)
    first, second = jax.random.split(key)
    counts = jax.random.randint(first, (N_DOM,), BCUT // 2, BCUT + 1)
    fullest = jax.random.randint(second, (), 0, N_DOM)
    return jnp.where(jnp.arange(N_DOM) == fullest, BCUT, counts).astype(jnp.int32)


def touch_ends(entries, stream_key, smallest, high):
    place = [jax.random.randint(jax.random.fold_in(stream_key, axis), (), 0, length) for axis, length in enumerate(entries.shape)]
    longest = entries.shape.index(max(entries.shape))
    beside = place[:longest] + [(place[longest] + 1) % entries.shape[longest]] + place[longest + 1:]
    return entries.at[tuple(place)].set(smallest).at[tuple(beside)].set(high)


def block_scale(own_key, extent, pieces, smallest, top_value):
    level, own = 1.0, jax.random.fold_in(own_key, 6)
    for axis_at, parts in pieces:
        heights = jnp.exp(jax.random.uniform(jax.random.fold_in(own, axis_at), (parts,), jnp.float32, smallest / len(pieces), top_value / len(pieces)))
        level = level * jnp.repeat(heights, extent[axis_at] // parts).reshape([-1 if axis == axis_at else 1 for axis in range(len(extent))])
    return level


def normal_values(own_key, extent, deviation, bound, shards=(), held_as=jnp.bfloat16):
    level = block_scale(own_key, extent, shards, -0.22, 0.18) if shards else 1.0
    values = jax.random.normal(own_key, extent, jnp.float32) * deviation * level
    return jnp.minimum(jnp.maximum(values, -bound), bound).astype(held_as)


def setup_inputs(seed: int = 0) -> dict:
    streams_of = jax.random.split(jax.random.key(seed), 17)
    return {
        "start_block": draw_start_block(jax.random.fold_in(streams_of[16], 71), 0),
        "prior_dirs": normal_values(streams_of[1], (M, NODES), 1.0, 6.0, ((0, 16), (1, 16)), jnp.float32),
        "degree": jnp.clip(jnp.exp(math.log(4.0) - 1.3862944 * jax.random.uniform(streams_of[2], (NODES,), jnp.float32) ** block_scale(streams_of[2], (NODES,), ((0, 16),), -0.2, 0.2)), 1.0, 4.0),
        "tiles": normal_values(streams_of[3], (TILES * N_DOM, TILE, TILE), ((TPR + CTR) * TILE) ** -0.5, 0.21875, ((0, 16),), jnp.float32),
        "tile_rows": touch_ends(jax.random.randint(streams_of[4], (TILES * N_DOM,), 0, NDEV // TILE), jax.random.fold_in(streams_of[4], 1), 0, (NDEV // TILE) - 1).astype(jnp.int32),
        "tile_cols": touch_ends(jax.random.randint(streams_of[5], (TILES * N_DOM,), 0, NDEV // TILE), jax.random.fold_in(streams_of[5], 1), 0, (NDEV // TILE) - 1).astype(jnp.int32),
        "cut_rows": touch_ends(jax.random.randint(streams_of[6], (BCUT * N_DOM,), 0, NDEV), jax.random.fold_in(streams_of[6], 1), 0, NDEV - 1).astype(jnp.int32),
        "cut_count": draw_cut_count(jax.random.fold_in(streams_of[16], 71), 0),
        "bound_tiles": normal_values(streams_of[8], (CT * N_DOM, TILE, TILE), ((TPR + CTR) * TILE) ** -0.5, 0.21875, ((0, 16),), jnp.float32),
        "bound_rows": touch_ends(jax.random.randint(streams_of[9], (CT * N_DOM,), 0, NDEV // TILE), jax.random.fold_in(streams_of[9], 1), 0, (NDEV // TILE) - 1).astype(jnp.int32),
        "bound_cols": touch_ends(jax.random.randint(streams_of[10], (CT * N_DOM,), 0, N_DOM * BCUT // TILE), jax.random.fold_in(streams_of[10], 1), 0, (N_DOM * BCUT // TILE) - 1).astype(jnp.int32),
        "rot_xx": normal_values(streams_of[11], (M, M), (3 * M) ** -0.5, 0.21875, (), jnp.float32),
        "rot_xr": normal_values(streams_of[12], (M, M), (3 * M) ** -0.5, 0.21875, (), jnp.float32),
        "rot_xp": normal_values(streams_of[13], (M, M), (3 * M) ** -0.5, 0.21875, (), jnp.float32),
        "rot_pr": normal_values(streams_of[14], (M, M), (2 * M) ** -0.5, 0.25, (), jnp.float32),
        "rot_pp": normal_values(streams_of[15], (M, M), (2 * M) ** -0.5, 0.25, (), jnp.float32),
    }


def tile_product(source, tile_set, row_ids, col_ids, blocks_out):
    width = source.shape[0]
    tile = tile_set.shape[1]
    blocks = source.reshape(width, -1, tile)
    picked = jnp.take(blocks, col_ids, axis=1)
    product = jnp.einsum('mtk,tjk->mtj', picked, tile_set, precision=lax.Precision.HIGHEST)
    onehot = (row_ids[:, None] == jnp.arange(blocks_out, dtype=jnp.int32)[None, :]).astype(jnp.float32)
    summed = jnp.einsum('mtj,tr->mrj', product, onehot, precision=lax.Precision.HIGHEST)
    return summed.reshape(width, blocks_out * tile)

def matmul(left, right):
    return jnp.dot(left, right, precision=lax.Precision.HIGHEST)

def normalize(values):
    sumsq = lax.optimization_barrier(jnp.sum(values * values, axis=1))
    return values / jnp.sqrt(sumsq / NODES + 1e-06)[:, None]

def reference(start_block, prior_dirs, degree, tiles, tile_rows, tile_cols, cut_rows, cut_count, bound_tiles, bound_rows, bound_cols, rot_xx, rot_xr, rot_xp, rot_pr, rot_pp):
    blocks_out = NDEV // TILE

    def operate(field):
        grouped = field.reshape(M, N_DOM, NDEV)
        cuts = cut_rows.reshape(N_DOM, BCUT)
        live = (jnp.arange(BCUT, dtype=jnp.int32)[None, :] < cut_count[:, None]).astype(jnp.float32)
        picked = jnp.take_along_axis(grouped, cuts[None, :, :], axis=2) * live[None, :, :]
        far = picked.reshape(M, N_DOM * BCUT)

        def one_group(group):
            own = lax.dynamic_slice_in_dim(field, group * NDEV, NDEV, 1)
            near = tile_product(own, lax.dynamic_slice_in_dim(tiles, group * TILES, TILES, 0), lax.dynamic_slice_in_dim(tile_rows, group * TILES, TILES, 0), lax.dynamic_slice_in_dim(tile_cols, group * TILES, TILES, 0), blocks_out)
            across = tile_product(far, lax.dynamic_slice_in_dim(bound_tiles, group * CT, CT, 0), lax.dynamic_slice_in_dim(bound_rows, group * CT, CT, 0), lax.dynamic_slice_in_dim(bound_cols, group * CT, CT, 0), blocks_out)
            diag = lax.dynamic_slice_in_dim(degree, group * NDEV, NDEV, 0)
            return diag[None, :] * own - (near + across)
        result = lax.map(one_group, jnp.arange(N_DOM, dtype=jnp.int32))
        return jnp.transpose(result, (1, 0, 2)).reshape(M, NODES)
    block = normalize(start_block)
    directions = prior_dirs
    ritz = jnp.zeros((M,), jnp.float32)
    for step in range(ITERS):
        image = operate(block)
        ritz = lax.optimization_barrier(jnp.sum(block * image, axis=1)) / lax.optimization_barrier(jnp.sum(block * block, axis=1))
        resid = image - ritz[:, None] * block
        rotated = matmul(rot_xx, block) + matmul(rot_xr, resid) + matmul(rot_xp, directions)
        directions = matmul(rot_pr, resid) + matmul(rot_pp, directions)
        block = normalize(rotated)
    return (block, directions, ritz)
```

```python
import functools

import jax
import jax.numpy as jnp
from jax import lax
from jax.experimental import pallas as pl
from jax.experimental.pallas import tpu as pltpu
from jax.sharding import PartitionSpec as P

ITERS = 4
MESH = pl.DeviceIdType.MESH
LANES = 128
HALF = 64


def split(value):
    high = value.astype(jnp.bfloat16)
    low = (value - high.astype(jnp.float32)).astype(jnp.bfloat16)
    return high, low


def swap(value):
    return pltpu.roll(value, HALF, value.ndim - 1)


def left_half(shape):
    return lax.broadcasted_iota(jnp.int32, shape, len(shape) - 1) < HALF


def kernel(
    nodes,
    start_hbm,
    prior_hbm,
    degree_hbm,
    tiles_hbm,
    trows_hbm,
    tcols_hbm,
    cuts_hbm,
    count_hbm,
    btiles_hbm,
    brows_hbm,
    bcols_hbm,
    xx_hbm,
    xr_hbm,
    xp_hbm,
    pr_hbm,
    pp_hbm,
    block_ref,
    dirs_ref,
    ritz_ref,
    start_ref,
    prior_ref,
    degree_ref,
    tiles_ref,
    trows,
    tcols,
    cuts_ref,
    count,
    btiles_ref,
    brows,
    bcols,
    rot_ref,
    load_sem,
    onehot,
    weights,
    bweights,
    rotcat,
    yblk,
    yst,
    xblk,
    acc,
    pdir,
    far_out,
    far_in,
    y_out,
    y_in,
    x_out,
    x_in,
    r_out,
    r_in,
    p_out,
    p_in,
    s_out,
    s_in,
    c_out,
    c_in,
    far_send,
    far_recv,
    y_send,
    y_recv,
    x_send,
    x_recv,
    r_send,
    r_recv,
    p_send,
    p_recv,
    s_send,
    s_recv,
    c_send,
    c_recv,
):
    dom, panel = lax.axis_index("dom"), lax.axis_index("panel")
    n_dom, n_panel = lax.axis_size("dom"), lax.axis_size("panel")
    blocks = yblk.shape[0]
    n_tiles, n_bound = weights.shape[0], bweights.shape[0]
    width = yblk.shape[1]

    loads = []

    def load(src, dst):
        copy = pltpu.make_async_copy(src, dst, load_sem.at[len(loads)])
        copy.start()
        loads.append(copy)
        return copy

    got_cuts = load(cuts_hbm, cuts_ref)
    got_count = load(count_hbm, count)
    got_start = load(start_hbm, start_ref)
    got_prior = load(prior_hbm, prior_ref)
    got_index = [
        load(trows_hbm, trows),
        load(tcols_hbm, tcols),
        load(brows_hbm, brows),
        load(bcols_hbm, bcols),
        load(degree_hbm, degree_ref),
    ]
    got_tiles = load(tiles_hbm, tiles_ref)
    got_btiles = load(btiles_hbm, btiles_ref)
    got_rot = [
        load(src, rot_ref.at[at])
        for at, src in enumerate((xx_hbm, xr_hbm, xp_hbm, pr_hbm, pp_hbm))
    ]

    barrier = pltpu.get_barrier_semaphore()
    for step in range(1, n_dom):
        pl.semaphore_signal(
            barrier, inc=1, device_id={"dom": (dom + step) % n_dom}, device_id_type=MESH
        )
    for step in range(1, n_panel):
        pl.semaphore_signal(
            barrier, inc=1, device_id={"panel": (panel + step) % n_panel}, device_id_type=MESH
        )

    def spread(axis, me, n, source, target, send, recv):
        for step in range(1, n):
            peer = (me + step) % n
            pltpu.make_async_remote_copy(
                src_ref=source(peer),
                dst_ref=target(me),
                send_sem=send,
                recv_sem=recv,
                device_id={axis: peer},
                device_id_type=MESH,
            ).start()

    def arrive(like, sem):
        pltpu.make_async_copy(like, like, sem).wait()

    eye = (
        lax.broadcasted_iota(jnp.int32, (width, LANES), 0)
        == lax.broadcasted_iota(jnp.int32, (width, LANES), 1)
    )

    def to_row(partial):
        column = jnp.sum(partial, axis=1, keepdims=True)
        return jnp.sum(jnp.where(eye, column, 0.0), axis=0, keepdims=True)

    def to_column(row):
        return jnp.sum(jnp.where(eye, row, 0.0), axis=1, keepdims=True)

    left8 = left_half((8, LANES))

    def cut_pieces(value):
        top, bottom = value[:8], value[8:]
        return (
            jnp.where(left8, top, swap(bottom)),
            jnp.where(left8, swap(top), bottom),
        )

    def send_panel(pieces_of, out, into, send, recv):
        for b in range(blocks):
            first, second = cut_pieces(pieces_of(b))
            out[2 * b] = first
            out[2 * b + 1] = second
        spread("panel", panel, n_panel, lambda q: out.at[q], lambda q: into.at[q], send, recv)
        into[panel] = out[panel]

    def unpack(into):
        got = into[...]
        turned = swap(got)
        left = left_half(got.shape)
        top = jnp.where(left, got, turned)
        bottom = jnp.where(left, turned, got)
        return jnp.concatenate([top[:, None], bottom[:, None]], axis=1).reshape(-1, LANES)

    def operand(value):
        high = value.astype(jnp.bfloat16).astype(jnp.float32)
        left = left_half(value.shape)
        both = jnp.where(left, high, value - high).astype(jnp.bfloat16)
        only = jnp.where(left, high, 0.0).astype(jnp.bfloat16)
        return jnp.concatenate([both, only], axis=0)

    def rotate(at, stacked):
        return jnp.dot(rotcat[at], stacked, preferred_element_type=jnp.float32)

    def pack(total, out):
        value = total + swap(total)
        value4 = value.reshape(n_panel, 2, 8, LANES)
        out[...] = jnp.where(left_half((n_panel, 8, LANES)), value4[:, 0], value4[:, 1])
        return value

    def assemble(into, put):
        for b in range(blocks):
            first, second = into[2 * b], into[2 * b + 1]
            top = jnp.where(left8, first, swap(second))
            bottom = jnp.where(left8, swap(first), second)
            put(b, jnp.concatenate([top, bottom], axis=0))

    def put_y(b, value):
        yblk[b] = value

    def send_dom(partial, out, into, send, recv):
        out[...] = to_row(partial)
        spread("dom", dom, n_dom, lambda q: out, lambda q: into.at[q], send, recv)
        into[dom] = out[...]

    def total_dom(into, recv):
        arrive(into.at[pl.ds(0, n_dom - 1)], recv)
        return jnp.sum(into[...], axis=0)

    def factor(sumsq):
        return jnp.sqrt(sumsq / nodes + 1e-06)

    got_cuts.wait()
    got_count.wait()
    n_cut = cuts_ref.shape[1]
    cut = jnp.where(
        lax.broadcasted_iota(jnp.int32, (1, n_cut), 1) < count[0], cuts_ref[...], -1
    )
    for b in range(blocks):
        row = lax.broadcasted_iota(jnp.int32, (LANES, n_cut), 0) + b * LANES
        onehot[pl.ds(b * LANES, LANES)] = (row == cut).astype(jnp.float32).astype(jnp.bfloat16)
    got_start.wait()
    for b in range(blocks):
        put_y(b, start_ref[:, b * LANES : (b + 1) * LANES])
    got_prior.wait()

    pl.semaphore_wait(barrier, n_dom + n_panel - 2)

    def tile_step(t, source, weight, row, totals):
        product = lax.dot_general(
            source, weight, (((1,), (1,)), ((), ())), preferred_element_type=jnp.float32
        )
        product = product[:width] + product[width:]
        return tuple(
            total + jnp.where(row == r, product, 0.0) for r, total in enumerate(totals)
        )

    def doubled(value):
        high, low = split(value)
        stacked = jnp.concatenate([high, low], axis=0)
        return jnp.concatenate([stacked, stacked], axis=1)

    def iterate(k, _):
        for b in range(blocks):
            yst[b] = doubled(yblk[b])
        chosen = jnp.zeros((2 * width, n_cut), jnp.float32)
        for b in range(blocks):
            chosen += jnp.dot(
                yst[b, :, :LANES],
                onehot[pl.ds(b * LANES, LANES)],
                preferred_element_type=jnp.float32,
            )
        chosen = chosen[:width] + chosen[width:]
        halves = n_cut // LANES
        for h in range(halves):
            far_out[k, h] = chosen[:, h * LANES : (h + 1) * LANES]
        spread(
            "dom",
            dom,
            n_dom,
            lambda q: far_out.at[k],
            lambda q: far_in.at[k, pl.ds(q * halves, halves)],
            far_send.at[k],
            far_recv.at[k],
        )
        far_in[k, pl.ds(dom * halves, halves)] = far_out[k]

        partial = jnp.zeros((width, LANES), jnp.float32)
        for b in range(blocks):
            partial += yblk[b] * yblk[b]
        send_dom(partial, s_out.at[k], s_in.at[k], s_send.at[k], s_recv.at[k])

        @pl.when(k == 0)
        def _():
            send_panel(
                lambda b: prior_ref[:, b * LANES : (b + 1) * LANES],
                p_out.at[0],
                p_in.at[0],
                p_send.at[0],
                p_recv.at[0],
            )
            for copy in got_index:
                copy.wait()
            got_tiles.wait()

            def prepare(t, _):
                high, low = split(tiles_ref[t])
                weights[t] = jnp.concatenate([high, low], axis=1)
                return 0

            lax.fori_loop(0, n_tiles, prepare, 0)

        def interior(t, totals):
            return tile_step(t, yst[tcols[t]], weights[t], trows[t], totals)

        totals = lax.fori_loop(
            0, n_tiles, interior, (jnp.zeros((width, LANES), jnp.float32),) * blocks
        )
        for b in range(blocks):
            acc[b] = totals[b]

        sumsq = total_dom(s_in.at[k], s_recv.at[k])
        scale = to_column(1.0 / factor(sumsq))
        for b in range(blocks):
            xblk[b] = yblk[b] * scale
        send_panel(lambda b: xblk[b], x_out.at[k], x_in.at[k], x_send.at[k], x_recv.at[k])

        @pl.when(k == 0)
        def _():
            got_btiles.wait()

            def prepare(t, _):
                high, low = split(btiles_ref[t])
                bweights[t] = jnp.concatenate([high, low], axis=1)
                return 0

            lax.fori_loop(0, n_bound, prepare, 0)
            for at, copy in enumerate(got_rot):
                copy.wait()
                high, low = split(rot_ref[at])
                rotcat[at] = jnp.concatenate([high, low], axis=1)
            arrive(p_in.at[0, pl.ds(0, n_panel - 1)], p_recv.at[0])
            pdir[...] = unpack(p_in.at[0])

        arrive(far_in.at[k, pl.ds(0, (n_dom - 1) * halves)], far_recv.at[k])

        def boundary(t, totals):
            source = doubled(far_in[k, bcols[t]])
            return tile_step(t, source, bweights[t], brows[t], totals)

        totals = lax.fori_loop(0, n_bound, boundary, tuple(acc[b] for b in range(blocks)))
        partial = jnp.zeros((width, LANES), jnp.float32)
        for b in range(blocks):
            image = degree_ref[:, b * LANES : (b + 1) * LANES] * yblk[b] - totals[b]
            acc[b] = image
            partial += yblk[b] * image
        send_dom(partial, c_out.at[k], c_in.at[k], c_send.at[k], c_recv.at[k])
        ritz = total_dom(c_in.at[k], c_recv.at[k]) / sumsq
        ritz_ref[...] = ritz
        column = to_column(ritz)
        send_panel(
            lambda b: acc[b] * scale - column * xblk[b],
            r_out.at[k],
            r_in.at[k],
            r_send.at[k],
            r_recv.at[k],
        )

        arrive(x_in.at[k, pl.ds(0, n_panel - 1)], x_recv.at[k])
        old = operand(pdir[...])
        base = rotate(0, operand(unpack(x_in.at[k]))) + rotate(2, old)
        arrive(r_in.at[k, pl.ds(0, n_panel - 1)], r_recv.at[k])
        resid = operand(unpack(r_in.at[k]))
        pack(base + rotate(1, resid), y_out.at[k])
        spread(
            "panel",
            panel,
            n_panel,
            lambda q: y_out.at[k, q],
            lambda q: y_in.at[k, q],
            y_send.at[k],
            y_recv.at[k],
        )
        y_in[k, panel] = y_out[k, panel]

        pdir[...] = pack(rotate(3, resid) + rotate(4, old), p_out.at[1])

        arrive(y_in.at[k, pl.ds(0, n_panel - 1)], y_recv.at[k])
        assemble(y_in.at[k], put_y)
        return 0

    lax.fori_loop(0, ITERS, iterate, 0)

    partial = jnp.zeros((width, LANES), jnp.float32)
    for b in range(blocks):
        partial += yblk[b] * yblk[b]
    send_dom(partial, s_out.at[ITERS], s_in.at[ITERS], s_send.at[ITERS], s_recv.at[ITERS])
    spread(
        "panel",
        panel,
        n_panel,
        lambda q: p_out.at[1, q],
        lambda q: p_in.at[1, q],
        p_send.at[1],
        p_recv.at[1],
    )
    p_in[1, panel] = p_out[1, panel]
    scale = to_column(1.0 / factor(total_dom(s_in.at[ITERS], s_recv.at[ITERS])))
    for b in range(blocks):
        block_ref[:, b * LANES : (b + 1) * LANES] = yblk[b] * scale
    arrive(p_in.at[1, pl.ds(0, n_panel - 1)], p_recv.at[1])

    def put_dirs(b, value):
        dirs_ref[:, b * LANES : (b + 1) * LANES] = value

    assemble(p_in.at[1], put_dirs)

    def left(n, like, sem):
        for _ in range(n - 1):
            arrive(like, sem)

    def drain(k, _):
        left(n_dom, far_out.at[k], far_send.at[k])
        left(n_dom, c_out.at[k], c_send.at[k])
        for out, sem in ((y_out, y_send), (x_out, x_send), (r_out, r_send)):
            arrive(out.at[k, pl.ds(0, n_panel - 1)], sem.at[k])
        return 0

    lax.fori_loop(0, ITERS, drain, 0)

    def drain_self(k, _):
        left(n_dom, s_out.at[k], s_send.at[k])
        return 0

    lax.fori_loop(0, ITERS + 1, drain_self, 0)
    for at in range(2):
        arrive(p_out.at[at, pl.ds(0, n_panel - 1)], p_send.at[at])


def local(n_dom, n_panel, *args):
    start, prior, degree, tiles, trows, tcols, cuts, count, btiles, brows, bcols = args[:11]
    width, ndev = start.shape
    blocks = ndev // LANES
    n_tiles, n_bound, n_cut = tiles.shape[0], btiles.shape[0], cuts.shape[0]
    rows = args[11].shape[0]
    f32, bf16, i32 = jnp.float32, jnp.bfloat16, jnp.int32
    vmem, dma = pltpu.VMEM, pltpu.SemaphoreType.DMA
    n = ITERS

    def smem(shape):
        return pltpu.SMEM(shape, i32)

    def pieces(count):
        return vmem((count, n_panel, 8, LANES), f32)

    scratch = [
        vmem((width, ndev), f32),
        vmem((width, ndev), f32),
        vmem((1, ndev), f32),
        vmem(tiles.shape, f32),
        smem(trows.shape),
        smem(tcols.shape),
        vmem((1, n_cut), i32),
        smem(count.shape),
        vmem(btiles.shape, f32),
        smem(brows.shape),
        smem(bcols.shape),
        vmem((5, rows, rows), f32),
        dma((16,)),
        vmem((ndev, n_cut), bf16),
        vmem((n_tiles, LANES, 2 * LANES), bf16),
        vmem((n_bound, LANES, 2 * LANES), bf16),
        vmem((5, rows, 2 * rows), bf16),
        vmem((blocks, width, LANES), f32),
        vmem((blocks, 2 * width, 2 * LANES), bf16),
        vmem((blocks, width, LANES), f32),
        vmem((blocks, width, LANES), f32),
        vmem((rows, LANES), f32),
        vmem((n, n_cut // LANES, width, LANES), f32),
        vmem((n, n_dom * n_cut // LANES, width, LANES), f32),
        pieces(n),
        pieces(n),
        pieces(n),
        pieces(n),
        pieces(n),
        pieces(n),
        pieces(2),
        pieces(2),
        vmem((n + 1, 1, LANES), f32),
        vmem((n + 1, n_dom, 1, LANES), f32),
        vmem((n, 1, LANES), f32),
        vmem((n, n_dom, 1, LANES), f32),
    ]
    for count_of in (n, n, n, n, 2, n + 1, n):
        scratch += [dma((count_of,)), dma((count_of,))]

    block, dirs, ritz = pl.pallas_call(
        functools.partial(kernel, ndev * n_dom),
        out_shape=(
            jax.ShapeDtypeStruct((width, ndev), f32),
            jax.ShapeDtypeStruct((width, ndev), f32),
            jax.ShapeDtypeStruct((1, LANES), f32),
        ),
        in_specs=[pl.BlockSpec(memory_space=pl.ANY)] * 16,
        out_specs=(pl.BlockSpec(memory_space=pltpu.VMEM),) * 3,
        scratch_shapes=scratch,
        compiler_params=pltpu.CompilerParams(
            collective_id=0, has_side_effects=True, vmem_limit_bytes=48 * 1024 * 1024
        ),
    )(
        start,
        prior,
        degree.reshape(1, -1),
        tiles,
        trows,
        tcols,
        cuts.reshape(1, -1),
        count,
        btiles,
        brows,
        bcols,
        *args[11:],
    )
    return block, dirs, ritz[0, :width]


def solution(mesh):
    return jax.shard_map(
        functools.partial(local, mesh.shape["dom"], mesh.shape["panel"]),
        mesh=mesh,
        in_specs=(
            P("panel", "dom"),
            P("panel", "dom"),
            P("dom"),
            P("dom", None, None),
            P("dom"),
            P("dom"),
            P("dom"),
            P("dom"),
            P("dom", None, None),
            P("dom"),
            P("dom"),
            P(),
            P(),
            P(),
            P(),
            P(),
        ),
        out_specs=(P("panel", "dom"), P("panel", "dom"), P("panel")),
        check_vma=False,
    )
```

```python
import functools

import jax
import jax.numpy as jnp
from jax import lax
from jax.experimental import pallas as pl
from jax.experimental.pallas import tpu as pltpu
from jax.sharding import PartitionSpec as P

ITERS = 4
MESH = pl.DeviceIdType.MESH
LANES = 128
HALF = 64
UNROLL = 8
K, Q = 0, 1
SHIFT = 2.5


def split(value):
    high = value.astype(jnp.bfloat16)
    low = (value - high.astype(jnp.float32)).astype(jnp.bfloat16)
    return high, low


def swap(value):
    return pltpu.roll(value, HALF, value.ndim - 1)


def left_half(shape):
    return lax.broadcasted_iota(jnp.int32, shape, len(shape) - 1) < HALF


def dot(left, right):
    return jnp.dot(left, right, preferred_element_type=jnp.float32)


def dot_transposed(left, right):
    return lax.dot_general(
        left, right, (((1,), (1,)), ((), ())), preferred_element_type=jnp.float32
    )


def kernel(
    nodes,
    start_hbm,
    prior_hbm,
    degree_hbm,
    tiles_hbm,
    trows_hbm,
    tcols_hbm,
    cuts_hbm,
    count_hbm,
    btiles_hbm,
    brows_hbm,
    bcols_hbm,
    xx_hbm,
    xr_hbm,
    xp_hbm,
    pr_hbm,
    pp_hbm,
    block_ref,
    dirs_ref,
    ritz_ref,
    start_ref,
    prior_ref,
    degree_ref,
    tiles_ref,
    trows,
    tcols,
    cuts_ref,
    count,
    btiles_ref,
    brows,
    bcols,
    rot_ref,
    load_sem,
    onehot,
    weights,
    bweights,
    xp_cat,
    pp_cat,
    y_cat,
    p_cat,
    field,
    stacked,
    acc,
    y_data,
    p_data,
    far_out,
    far_in,
    move_out,
    move_in,
    sum_out,
    sum_in,
    far_send,
    far_recv,
    move_send,
    move_recv,
    sum_send,
    sum_recv,
):
    dom, panel = lax.axis_index("dom"), lax.axis_index("panel")
    n_dom, n_panel = lax.axis_size("dom"), lax.axis_size("panel")
    blocks, width = field.shape[1], field.shape[2]
    n_tiles, n_bound = weights.shape[0], bweights.shape[0]
    rows = rot_ref.shape[1]
    n_cut = cuts_ref.shape[1]
    halves = n_cut // LANES
    f32, bf16 = jnp.float32, jnp.bfloat16

    loads = []

    def load(src, dst):
        copy = pltpu.make_async_copy(src, dst, load_sem.at[len(loads)])
        copy.start()
        loads.append(copy)
        return copy

    got_cuts = load(cuts_hbm, cuts_ref)
    got_count = load(count_hbm, count)
    got_start = load(start_hbm, start_ref)
    got_prior = load(prior_hbm, prior_ref)
    got_index = [
        load(trows_hbm, trows),
        load(tcols_hbm, tcols),
        load(brows_hbm, brows),
        load(bcols_hbm, bcols),
        load(degree_hbm, degree_ref),
    ]
    got_tiles = load(tiles_hbm, tiles_ref)
    got_btiles = load(btiles_hbm, btiles_ref)
    got_rot = [
        load(src, rot_ref.at[at])
        for at, src in enumerate((xx_hbm, xr_hbm, xp_hbm, pr_hbm, pp_hbm))
    ]

    barrier = pltpu.get_barrier_semaphore()
    for step in range(1, n_dom):
        pl.semaphore_signal(
            barrier, inc=1, device_id={"dom": (dom + step) % n_dom}, device_id_type=MESH
        )
    for step in range(1, n_panel):
        pl.semaphore_signal(
            barrier, inc=1, device_id={"panel": (panel + step) % n_panel}, device_id_type=MESH
        )

    def spread(axis, source, target, send, recv):
        me, n = (dom, n_dom) if axis == "dom" else (panel, n_panel)
        for step in range(1, n):
            peer = (me + step) % n
            pltpu.make_async_remote_copy(
                src_ref=source(peer),
                dst_ref=target(me),
                send_sem=send,
                recv_sem=recv,
                device_id={axis: peer},
                device_id_type=MESH,
            ).start()

    def arrive(like, sem):
        pltpu.make_async_copy(like, like, sem).wait()


    def set_block(kind, b, value):
        field[kind, b] = value
        high, low = split(value)
        both = jnp.concatenate([high, low], axis=0)
        at = kind * 2 * width
        stacked[b, at : at + 2 * width] = jnp.concatenate([both, both], axis=1)

    def send_far(kind, j):
        at = kind * 2 * width
        chosen = jnp.zeros((2 * width, n_cut), f32)
        for b in range(blocks):
            chosen += dot(
                stacked[b, at : at + 2 * width, :LANES], onehot[b * LANES : (b + 1) * LANES]
            )
        chosen = chosen[:width] + chosen[width:]
        slot = 2 * j + kind
        for h in range(halves):
            far_out[slot, h] = chosen[:, h * LANES : (h + 1) * LANES]
        spread(
            "dom",
            lambda q: far_out.at[slot],
            lambda q: far_in[slot].at[pl.ds(q * halves, halves)],
            far_send.at[slot],
            far_recv.at[slot],
        )
        far_in[slot][pl.ds(dom * halves, halves)] = far_out[slot]

    def collect(totals, products, row_ids):
        totals = list(totals)
        for product, row in zip(products, row_ids):
            for r in range(blocks):
                totals[r] = totals[r] + jnp.where(row == r, product, 0.0)
        return tuple(totals)

    def interior(kinds):
        wide = 2 * width * len(kinds)

        def step(i, totals):
            products, row_ids = [], []
            for u in range(min(UNROLL, n_tiles)):
                t = i * min(UNROLL, n_tiles) + u
                product = dot_transposed(stacked[tcols[t], :wide], weights[t])
                parts = [
                    product[2 * width * n : 2 * width * n + width]
                    + product[2 * width * n + width : 2 * width * (n + 1)]
                    for n in range(len(kinds))
                ]
                products.append(jnp.concatenate(parts, axis=0))
                row_ids.append(trows[t])
            return collect(totals, products, row_ids)

        zero = jnp.zeros((width * len(kinds), LANES), f32)
        totals = lax.fori_loop(0, n_tiles // min(UNROLL, n_tiles), step, (zero,) * blocks)
        for b in range(blocks):
            for n in range(len(kinds)):
                acc[n, b] = totals[b][n * width : (n + 1) * width]

    def boundary(kind, j):
        slot = 2 * j + kind
        arrive(far_in[slot].at[pl.ds(0, (n_dom - 1) * halves)], far_recv.at[slot])

        def step(i, totals):
            products, row_ids = [], []
            for u in range(min(UNROLL, n_bound)):
                t = i * min(UNROLL, n_bound) + u
                high, low = split(far_in[slot][bcols[t]])
                both = jnp.concatenate([high, low], axis=0)
                product = dot_transposed(jnp.concatenate([both, both], axis=1), bweights[t])
                products.append(product[:width] + product[width:])
                row_ids.append(brows[t])
            return collect(totals, products, row_ids)

        totals = lax.fori_loop(
            0,
            n_bound // min(UNROLL, n_bound),
            step,
            tuple(acc[kind, b] for b in range(blocks)),
        )
        return [
            (degree_ref[:, b * LANES : (b + 1) * LANES] - SHIFT) * field[kind, b] - totals[b]
            for b in range(blocks)
        ]

    left8 = left_half((8, LANES))

    def send_nodes(slot, values):
        for b in range(blocks):
            value = values(b)
            top, bottom = value[:8], value[8:]
            move_out[slot, 2 * b] = jnp.where(left8, top, swap(bottom))
            move_out[slot, 2 * b + 1] = jnp.where(left8, swap(top), bottom)
        move(slot)

    def move(slot):
        spread(
            "panel",
            lambda q: move_out.at[slot, q],
            lambda q: move_in.at[slot, q],
            move_send.at[slot],
            move_recv.at[slot],
        )
        move_in[slot, panel] = move_out[slot, panel]

    def wait_move(slot):
        arrive(move_in.at[slot, pl.ds(0, n_panel - 1)], move_recv.at[slot])

    def assemble(slot, put):
        for b in range(blocks):
            first, second = move_in[slot, 2 * b], move_in[slot, 2 * b + 1]
            top = jnp.where(left8, first, swap(second))
            bottom = jnp.where(left8, swap(first), second)
            put(b, jnp.concatenate([top, bottom], axis=0))


    def unpack(slot):
        got = move_in[slot]
        turned = swap(got)
        left = left_half(got.shape)
        top = jnp.where(left, got, turned)
        bottom = jnp.where(left, turned, got)
        return jnp.concatenate([top[:, None], bottom[:, None]], axis=1).reshape(rows, LANES)

    left_rows = left_half((rows, LANES))

    def put_operand(data, at, j, value):
        high = value.astype(bf16).astype(f32)
        lanes = slice(j * LANES, (j + 1) * LANES)
        data[at, :rows, lanes] = jnp.where(left_rows, high, value - high).astype(bf16)
        data[at, rows:, lanes] = jnp.where(left_rows, high, 0.0).astype(bf16)

    def receive(data, slot, j):
        wait_move(slot)
        put_operand(data, 0, j, unpack(slot))

    def put_matrix(ref, at, matrix):
        high, low = split(matrix)
        ref[:, at * 2 * rows : at * 2 * rows + rows] = high
        ref[:, at * 2 * rows + rows : (at + 1) * 2 * rows] = low

    def rotate(matrices, from_cat, k, first, count):
        now = k % 2
        lo, hi = first * LANES, (first + count) * LANES
        total = dot(matrices[:, : 2 * rows], y_data[now, :, lo:hi])
        total += dot(matrices[:, 2 * rows :], y_data[now, :, lo + LANES : hi + LANES])
        total += dot(from_cat[...], p_data[now, :, lo:hi])
        values = []
        for n in range(count):
            part = total[:, n * LANES : (n + 1) * LANES]
            values.append(part + swap(part))
        return values

    def pack(slot, value):
        value4 = value.reshape(n_panel, 2, 8, LANES)
        move_out[slot] = jnp.where(
            left_half((n_panel, 8, LANES)), value4[:, 0], value4[:, 1]
        )


    def send_sum(axis, slot, value):
        sum_out[slot] = value
        spread(
            axis,
            lambda q: sum_out.at[slot],
            lambda q: sum_in.at[slot, q],
            sum_send.at[slot],
            sum_recv.at[slot],
        )
        sum_in[slot, dom if axis == "dom" else panel] = value

    def wait_sum(axis, slot):
        n = n_dom if axis == "dom" else n_panel
        arrive(sum_in.at[slot, pl.ds(0, n - 1)], sum_recv.at[slot])
        return jnp.sum(sum_in[slot, :n], axis=0)

    own = lax.broadcasted_iota(jnp.int32, (width, rows), 1) == (
        lax.broadcasted_iota(jnp.int32, (width, rows), 0) + panel * width
    )

    def to_row(partial):
        column = jnp.sum(partial, axis=1, keepdims=True)
        return jnp.sum(jnp.where(own, column, 0.0), axis=0, keepdims=True)

    def to_column(row):
        return jnp.sum(jnp.where(own, row, 0.0), axis=1, keepdims=True)

    pick_row = lax.broadcasted_iota(jnp.int32, (width, 2 * LANES), 0)
    pick_lane = lax.broadcasted_iota(jnp.int32, (width, 2 * LANES), 1) // HALF % 2
    pick = (pick_row == pick_lane).astype(f32).astype(bf16)

    def node_sums(first, second):
        product = first * jnp.where(left_rows, first, second)
        high, low = split(product)
        return dot_transposed(pick, jnp.concatenate([high, low], axis=1))[:2]

    def inverse_factor(total):
        return 1.0 / jnp.sqrt(total[0:1] / nodes + 1e-06)


    got_cuts.wait()
    got_count.wait()
    cut = jnp.where(
        lax.broadcasted_iota(jnp.int32, (1, n_cut), 1) < count[0], cuts_ref[...], -1
    )
    for b in range(blocks):
        row = lax.broadcasted_iota(jnp.int32, (LANES, n_cut), 0) + b * LANES
        onehot[b * LANES : (b + 1) * LANES] = (row == cut).astype(f32).astype(bf16)
    got_start.wait()
    for b in range(blocks):
        set_block(K, b, start_ref[:, b * LANES : (b + 1) * LANES])
    got_prior.wait()
    for b in range(blocks):
        set_block(Q, b, prior_ref[:, b * LANES : (b + 1) * LANES])

    pl.semaphore_wait(barrier, n_dom + n_panel - 2)

    send_far(K, 0)
    send_far(Q, 0)
    send_nodes(0, lambda b: field[K, b])
    send_nodes(1, lambda b: field[Q, b])

    def split_tiles(source, target):
        def step(t, _):
            high, low = split(source[t])
            target[t] = jnp.concatenate([high, low], axis=1)
            return 0

        lax.fori_loop(0, source.shape[0], step, 0)

    for copy in got_index:
        copy.wait()
    got_tiles.wait()
    split_tiles(tiles_ref, weights)
    got_btiles.wait()
    split_tiles(btiles_ref, bweights)
    interior((K, Q))

    def advance(kind, j):
        images = boundary(kind, j)
        if kind == K and j == 0:
            square = jnp.zeros((width, LANES), f32)
            cross = jnp.zeros((width, LANES), f32)
            for b in range(blocks):
                square += field[K, b] * field[K, b]
                cross += field[K, b] * images[b]
            send_sum("dom", 0, jnp.concatenate([to_row(square), to_row(cross)], axis=0))
        for b in range(blocks):
            set_block(kind, b, images[b])
        if j + 1 < ITERS - kind:
            send_far(kind, j + 1)
        send_nodes(2 * (j + 1) + kind, lambda b: field[kind, b])

    advance(K, 0)
    advance(Q, 0)
    interior((K, Q))
    for copy in got_rot:
        copy.wait()
    put_matrix(xp_cat, 0, rot_ref[2])
    put_matrix(pp_cat, 0, rot_ref[4])
    receive(y_data, 0, 0)
    receive(p_data, 1, 0)
    send_sum("panel", 1, wait_sum("dom", 0))
    receive(y_data, 2, 1)
    receive(p_data, 3, 1)
    advance(K, 1)
    advance(Q, 1)

    f_block, f_dirs = 2 * ITERS + 1, 2 * ITERS + 2
    for k in range(ITERS):
        depth = ITERS - k
        slot = 2 * k + 1
        total = wait_sum("panel" if k == 0 else "dom", slot)
        scale = inverse_factor(total)
        ritz = total[1:2] / total[0:1]
        xr_scaled = rot_ref[1] * scale
        put_matrix(y_cat, 0, rot_ref[0] * scale - xr_scaled * ritz)
        put_matrix(y_cat, 1, xr_scaled)
        if k == 0:
            receive(y_data, 4, 2)
        now = rotate(y_cat, xp_cat, k, 0, min(2, depth))
        nxt = (k + 1) % 2
        if depth > 1:
            send_sum("panel", slot + 1, node_sums(now[0], now[1]))
            for n in range(2):
                put_operand(y_data, nxt, n, now[n])
        else:
            send_sum("panel", slot + 1, node_sums(now[0], now[0]))
            pack(f_block, now[0])
            move(f_block)
        pr_scaled = rot_ref[3] * scale
        put_matrix(p_cat, 0, -pr_scaled * ritz)
        put_matrix(p_cat, 1, pr_scaled)
        if depth > 1:
            first = rotate(p_cat, pp_cat, k, 0, min(2, depth - 1))
            for n, value in enumerate(first):
                put_operand(p_data, nxt, n, value)
        else:
            pack(f_dirs, rotate(p_cat, pp_cat, k, 0, 1)[0])
            move(f_dirs)
        if k == 0:
            interior((K, Q))
            advance(K, 2)
            advance(Q, 2)
            receive(p_data, 5, 2)
            receive(y_data, 6, 3)
            receive(p_data, 7, 3)
        if depth > 2:
            if k == 0:
                send_sum("dom", slot + 2, wait_sum("panel", slot + 1))
                interior((K,))
                advance(K, 3)
                receive(y_data, 8, 4)
            for n in range(2, depth):
                put_operand(y_data, nxt, n, rotate(y_cat, xp_cat, k, n, 1)[0])
            for n in range(2, depth - 1):
                put_operand(p_data, nxt, n, rotate(p_cat, pp_cat, k, n, 1)[0])
        if k > 0:
            send_sum("dom", slot + 2, wait_sum("panel", slot + 1))

    ritz_column = to_column(ritz + SHIFT)
    narrow = lax.broadcasted_iota(jnp.int32, (width, LANES), 1) == lax.broadcasted_iota(
        jnp.int32, (width, LANES), 0
    )
    ritz_ref[...] = jnp.sum(jnp.where(narrow, ritz_column, 0.0), axis=0, keepdims=True)

    def put_dirs(b, value):
        dirs_ref[:, b * LANES : (b + 1) * LANES] = value

    wait_move(f_dirs)
    assemble(f_dirs, put_dirs)
    wait_move(f_block)
    scale = to_column(inverse_factor(wait_sum("dom", 2 * ITERS + 1)))

    def put_block(b, value):
        block_ref[:, b * LANES : (b + 1) * LANES] = value * scale

    assemble(f_block, put_block)

    def drain(out, sem, n, whole):
        def step(slot, _):
            if whole:
                for _ in range(n - 1):
                    arrive(out.at[slot], sem.at[slot])
            else:
                arrive(out.at[slot, pl.ds(0, n - 1)], sem.at[slot])
            return 0

        lax.fori_loop(0, out.shape[0], step, 0)

    drain(far_out, far_send, n_dom, True)
    drain(move_out, move_send, n_panel, False)
    for slot in range(2 * ITERS + 2):
        n = n_panel if slot in (1, 2, 4, 6, 8) else n_dom
        for _ in range(n - 1):
            arrive(sum_out.at[slot], sum_send.at[slot])


def local(n_dom, n_panel, *args):
    start, prior, degree, tiles, trows, tcols, cuts, count, btiles, brows, bcols = args[:11]
    width, ndev = start.shape
    blocks = ndev // LANES
    n_tiles, n_bound, n_cut = tiles.shape[0], btiles.shape[0], cuts.shape[0]
    rows = args[11].shape[0]
    f32, bf16, i32 = jnp.float32, jnp.bfloat16, jnp.int32
    vmem, dma = pltpu.VMEM, pltpu.SemaphoreType.DMA
    n_far, n_move, n_sum = 2 * ITERS - 1, 2 * ITERS + 3, 2 * ITERS + 2

    def smem(shape):
        return pltpu.SMEM(shape, i32)

    scratch = [
        vmem((width, ndev), f32),
        vmem((width, ndev), f32),
        vmem((1, ndev), f32),
        vmem(tiles.shape, f32),
        smem(trows.shape),
        smem(tcols.shape),
        vmem((1, n_cut), i32),
        smem(count.shape),
        vmem(btiles.shape, f32),
        smem(brows.shape),
        smem(bcols.shape),
        vmem((5, rows, rows), f32),
        dma((16,)),
        vmem((ndev, n_cut), bf16),
        vmem((n_tiles, LANES, 2 * LANES), bf16),
        vmem((n_bound, LANES, 2 * LANES), bf16),
        vmem((rows, 2 * rows), bf16),
        vmem((rows, 2 * rows), bf16),
        vmem((rows, 4 * rows), bf16),
        vmem((rows, 4 * rows), bf16),
        vmem((2, blocks, width, LANES), f32),
        vmem((blocks, 4 * width, 2 * LANES), bf16),
        vmem((2, blocks, width, LANES), f32),
        vmem((2, 2 * rows, (ITERS + 1) * LANES), bf16),
        vmem((2, 2 * rows, ITERS * LANES), bf16),
        vmem((n_far, n_cut // LANES, width, LANES), f32),
        (vmem((n_dom * n_cut // LANES, width, LANES), f32),) * n_far,
        vmem((n_move, n_panel, 8, LANES), f32),
        vmem((n_move, n_panel, 8, LANES), f32),
        vmem((n_sum, 2, rows), f32),
        vmem((n_sum, max(n_dom, n_panel), 2, rows), f32),
    ]
    for slots in (n_far, n_move, n_sum):
        scratch += [dma((slots,)), dma((slots,))]

    block, dirs, ritz = pl.pallas_call(
        functools.partial(kernel, ndev * n_dom),
        out_shape=(
            jax.ShapeDtypeStruct((width, ndev), f32),
            jax.ShapeDtypeStruct((width, ndev), f32),
            jax.ShapeDtypeStruct((1, LANES), f32),
        ),
        in_specs=[pl.BlockSpec(memory_space=pl.ANY)] * 16,
        out_specs=(pl.BlockSpec(memory_space=pltpu.VMEM),) * 3,
        scratch_shapes=scratch,
        compiler_params=pltpu.CompilerParams(
            collective_id=0, has_side_effects=True, vmem_limit_bytes=60 * 1024 * 1024
        ),
    )(
        start,
        prior,
        degree.reshape(1, -1),
        tiles,
        trows,
        tcols,
        cuts.reshape(1, -1),
        count,
        btiles,
        brows,
        bcols,
        *args[11:],
    )
    return block, dirs, ritz[0, :width]


def solution(mesh):
    return jax.shard_map(
        functools.partial(local, mesh.shape["dom"], mesh.shape["panel"]),
        mesh=mesh,
        in_specs=(
            P("panel", "dom"),
            P("panel", "dom"),
            P("dom"),
            P("dom", None, None),
            P("dom"),
            P("dom"),
            P("dom"),
            P("dom"),
            P("dom", None, None),
            P("dom"),
            P("dom"),
            P(),
            P(),
            P(),
            P(),
            P(),
        ),
        out_specs=(P("panel", "dom"), P("panel", "dom"), P("panel")),
        check_vma=False,
    )
```

```python
import functools
import math

import jax
import jax.numpy as jnp
from jax import lax
from jax.experimental import pallas as pl
from jax.experimental.pallas import tpu as pltpu
from jax.sharding import PartitionSpec as P

ITERS = 4
MESH = pl.DeviceIdType.MESH
LANES = 128
HALF = 64
UNROLL = 16
K, Q = 0, 1
SHIFT = 2.5


def split(value):
    high = value.astype(jnp.bfloat16)
    low = (value - high.astype(jnp.float32)).astype(jnp.bfloat16)
    return high, low


def swap(value):
    return pltpu.roll(value, HALF, value.ndim - 1)


def left_half(shape):
    return lax.broadcasted_iota(jnp.int32, shape, len(shape) - 1) < HALF


def dot(left, right):
    return jnp.dot(left, right, preferred_element_type=jnp.float32)


def dot_transposed(left, right):
    return lax.dot_general(
        left, right, (((1,), (1,)), ((), ())), preferred_element_type=jnp.float32
    )


def kernel(
    nodes,
    start_hbm,
    prior_hbm,
    degree_hbm,
    tiles_hbm,
    trows_hbm,
    tcols_hbm,
    cuts_hbm,
    count_hbm,
    btiles_hbm,
    brows_hbm,
    bcols_hbm,
    xx_hbm,
    xr_hbm,
    xp_hbm,
    pr_hbm,
    pp_hbm,
    block_ref,
    dirs_ref,
    ritz_ref,
    start_ref,
    prior_ref,
    degree_ref,
    tiles_ref,
    trows,
    tcols,
    cuts_ref,
    count,
    btiles_ref,
    brows,
    bcols,
    rot_ref,
    load_sem,
    onehot,
    weights,
    bweights,
    xp_cat,
    pp_cat,
    y_cat,
    p_cat,
    field,
    stacked,
    acc,
    y_data,
    p_data,
    far_out,
    far_in,
    move_out,
    move_in,
    sum_out,
    sum_in,
    far_send,
    far_recv,
    move_send,
    move_recv,
    sum_send,
    sum_recv,
):
    dom, panel = lax.axis_index("dom"), lax.axis_index("panel")
    n_dom, n_panel = lax.axis_size("dom"), lax.axis_size("panel")
    blocks, width = field.shape[1], field.shape[2]
    n_tiles, n_bound = weights.shape[0], bweights.shape[0]
    rows = rot_ref.shape[1]
    n_cut = cuts_ref.shape[1]
    halves = n_cut // LANES
    f32, bf16 = jnp.float32, jnp.bfloat16

    side = math.isqrt(n_dom)
    dom_y, dom_x = dom // side, dom % side
    panel_z, core = panel // 2, panel % 2
    dom_steps = [(y, x) for y in range(n_dom // side) for x in range(side)][1:]
    dom_steps.sort(key=lambda s: -min(s[0], n_dom // side - s[0]) - min(s[1], side - s[1]))
    panel_steps = [(z, c) for z in range(n_panel // 2) for c in range(2)][1:]
    panel_steps.sort(key=lambda s: -min(s[0], n_panel // 2 - s[0]))
    peers = {
        "dom": [
            (dom_y + y) % (n_dom // side) * side + (dom_x + x) % side for y, x in dom_steps
        ],
        "panel": [(panel_z + z) % (n_panel // 2) * 2 + (core + c) % 2 for z, c in panel_steps],
    }

    barrier = pltpu.get_barrier_semaphore()
    for axis in ("dom", "panel"):
        for peer in peers[axis]:
            pl.semaphore_signal(barrier, inc=1, device_id={axis: peer}, device_id_type=MESH)

    loads = []

    def load(src, dst):
        copy = pltpu.make_async_copy(src, dst, load_sem.at[len(loads)])
        copy.start()
        loads.append(copy)
        return copy

    got_cuts = load(cuts_hbm, cuts_ref)
    got_count = load(count_hbm, count)
    got_start = load(start_hbm, start_ref)
    got_prior = load(prior_hbm, prior_ref)
    got_index = [
        load(trows_hbm, trows),
        load(tcols_hbm, tcols),
        load(brows_hbm, brows),
        load(bcols_hbm, bcols),
        load(degree_hbm, degree_ref),
    ]
    got_tiles = load(tiles_hbm, tiles_ref)
    got_btiles = load(btiles_hbm, btiles_ref)
    got_rot = [
        load(src, rot_ref.at[at])
        for at, src in enumerate((xx_hbm, xr_hbm, xp_hbm, pr_hbm, pp_hbm))
    ]

    def spread(axis, source, target, send, recv):
        me = dom if axis == "dom" else panel
        for peer in peers[axis]:
            pltpu.make_async_remote_copy(
                src_ref=source(peer),
                dst_ref=target(me),
                send_sem=send,
                recv_sem=recv,
                device_id={axis: peer},
                device_id_type=MESH,
            ).start()

    def arrive(like, sem):
        pltpu.make_async_copy(like, like, sem).wait()


    def set_block(kind, b, value):
        field[kind, b] = value
        high, low = split(value)
        both = jnp.concatenate([high, low], axis=0)
        at = kind * 2 * width
        stacked[b, at : at + 2 * width] = jnp.concatenate([both, both], axis=1)

    def choose(kind, j):
        at = kind * 2 * width
        chosen = jnp.zeros((2 * width, n_cut), f32)
        for b in range(blocks):
            chosen += dot(
                stacked[b, at : at + 2 * width, :LANES], onehot[b * LANES : (b + 1) * LANES]
            )
        chosen = chosen[:width] + chosen[width:]
        slot = 2 * j + kind
        for h in range(halves):
            far_out[slot, h] = chosen[:, h * LANES : (h + 1) * LANES]

    def send_far(kind, j):
        slot = 2 * j + kind
        spread(
            "dom",
            lambda q: far_out.at[slot],
            lambda q: far_in[slot].at[pl.ds(q * halves, halves)],
            far_send.at[slot],
            far_recv.at[slot],
        )
        far_in[slot][pl.ds(dom * halves, halves)] = far_out[slot]

    def collect(totals, products, row_ids):
        totals = list(totals)
        for product, row in zip(products, row_ids):
            for r in range(blocks):
                totals[r] = totals[r] + jnp.where(row == r, product, 0.0)
        return tuple(totals)

    def interior(kinds):
        wide = 2 * width * len(kinds)

        def step(i, totals):
            products, row_ids = [], []
            for u in range(min(UNROLL, n_tiles)):
                t = i * min(UNROLL, n_tiles) + u
                product = dot_transposed(stacked[tcols[t], :wide], weights[t])
                parts = [
                    product[2 * width * n : 2 * width * n + width]
                    + product[2 * width * n + width : 2 * width * (n + 1)]
                    for n in range(len(kinds))
                ]
                products.append(jnp.concatenate(parts, axis=0))
                row_ids.append(trows[t])
            return collect(totals, products, row_ids)

        zero = jnp.zeros((width * len(kinds), LANES), f32)
        totals = lax.fori_loop(0, n_tiles // min(UNROLL, n_tiles), step, (zero,) * blocks)
        for b in range(blocks):
            for n in range(len(kinds)):
                acc[n, b] = totals[b][n * width : (n + 1) * width]

    def boundary(kind, j):
        slot = 2 * j + kind
        arrive(far_in[slot].at[pl.ds(0, (n_dom - 1) * halves)], far_recv.at[slot])

        def step(i, totals):
            products, row_ids = [], []
            for u in range(min(UNROLL, n_bound)):
                t = i * min(UNROLL, n_bound) + u
                high, low = split(far_in[slot][bcols[t]])
                both = jnp.concatenate([high, low], axis=0)
                product = dot_transposed(jnp.concatenate([both, both], axis=1), bweights[t])
                products.append(product[:width] + product[width:])
                row_ids.append(brows[t])
            return collect(totals, products, row_ids)

        totals = lax.fori_loop(
            0,
            n_bound // min(UNROLL, n_bound),
            step,
            tuple(acc[kind, b] for b in range(blocks)),
        )
        return [
            (degree_ref[:, b * LANES : (b + 1) * LANES] - SHIFT) * field[kind, b] - totals[b]
            for b in range(blocks)
        ]

    left8 = left_half((8, LANES))

    def send_nodes(slot, values):
        for b in range(blocks):
            value = values(b)
            top, bottom = value[:8], value[8:]
            move_out[slot, 2 * b] = jnp.where(left8, top, swap(bottom))
            move_out[slot, 2 * b + 1] = jnp.where(left8, swap(top), bottom)
        move(slot)

    def move(slot):
        spread(
            "panel",
            lambda q: move_out.at[slot, q],
            lambda q: move_in.at[slot, q],
            move_send.at[slot],
            move_recv.at[slot],
        )
        move_in[slot, panel] = move_out[slot, panel]

    def wait_move(slot):
        arrive(move_in.at[slot, pl.ds(0, n_panel - 1)], move_recv.at[slot])

    def assemble(slot, put):
        for b in range(blocks):
            first, second = move_in[slot, 2 * b], move_in[slot, 2 * b + 1]
            top = jnp.where(left8, first, swap(second))
            bottom = jnp.where(left8, swap(first), second)
            put(b, jnp.concatenate([top, bottom], axis=0))


    def unpack(slot):
        got = move_in[slot]
        turned = swap(got)
        left = left_half(got.shape)
        top = jnp.where(left, got, turned)
        bottom = jnp.where(left, turned, got)
        return jnp.concatenate([top[:, None], bottom[:, None]], axis=1).reshape(rows, LANES)

    left_rows = left_half((rows, LANES))

    def put_operand(data, at, j, value):
        high = value.astype(bf16).astype(f32)
        lanes = slice(j * LANES, (j + 1) * LANES)
        data[at, :rows, lanes] = jnp.where(left_rows, high, value - high).astype(bf16)
        data[at, rows:, lanes] = jnp.where(left_rows, high, 0.0).astype(bf16)

    def receive(data, slot, j):
        wait_move(slot)
        put_operand(data, 0, j, unpack(slot))

    def put_matrix(ref, at, matrix):
        high, low = split(matrix)
        ref[:, at * 2 * rows : at * 2 * rows + rows] = high
        ref[:, at * 2 * rows + rows : (at + 1) * 2 * rows] = low

    def scale_matrices(k, total):
        scale = inverse_factor(total)
        ritz = total[1:2] / total[0:1]
        xr_scaled = rot_ref[1] * scale
        put_matrix(y_cat.at[k % 2], 0, rot_ref[0] * scale - xr_scaled * ritz)
        put_matrix(y_cat.at[k % 2], 1, xr_scaled)
        return scale, ritz

    def scale_direction_matrices(scale, ritz):
        pr_scaled = rot_ref[3] * scale
        put_matrix(p_cat, 0, -pr_scaled * ritz)
        put_matrix(p_cat, 1, pr_scaled)

    def new_y(k, first, count):
        return rotate(y_cat.at[k % 2], xp_cat, k, first, count)

    def new_p(k, first, count):
        return rotate(p_cat, pp_cat, k, first, count)

    def put_y(k, first, values):
        for n, value in enumerate(values):
            put_operand(y_data, (k + 1) % 2, first + n, value)

    def put_p(k, first, values):
        for n, value in enumerate(values):
            put_operand(p_data, (k + 1) % 2, first + n, value)

    def rotate(matrices, from_cat, k, first, count):
        now = k % 2
        lo, hi = first * LANES, (first + count) * LANES
        total = dot(matrices[:, : 2 * rows], y_data[now, :, lo:hi])
        total += dot(matrices[:, 2 * rows :], y_data[now, :, lo + LANES : hi + LANES])
        total += dot(from_cat[...], p_data[now, :, lo:hi])
        values = []
        for n in range(count):
            part = total[:, n * LANES : (n + 1) * LANES]
            values.append(part + swap(part))
        return values

    def pack(slot, value):
        value4 = value.reshape(n_panel, 2, 8, LANES)
        move_out[slot] = jnp.where(
            left_half((n_panel, 8, LANES)), value4[:, 0], value4[:, 1]
        )


    def send_sum(axis, slot, value):
        sum_out[slot] = value
        spread(
            axis,
            lambda q: sum_out.at[slot],
            lambda q: sum_in.at[slot, q],
            sum_send.at[slot],
            sum_recv.at[slot],
        )
        sum_in[slot, dom if axis == "dom" else panel] = value

    def wait_sum(axis, slot):
        n = n_dom if axis == "dom" else n_panel
        arrive(sum_in.at[slot, pl.ds(0, n - 1)], sum_recv.at[slot])
        return jnp.sum(sum_in[slot, :n], axis=0)

    own = lax.broadcasted_iota(jnp.int32, (width, rows), 1) == (
        lax.broadcasted_iota(jnp.int32, (width, rows), 0) + panel * width
    )

    def to_row(partial):
        column = jnp.sum(partial, axis=1, keepdims=True)
        return jnp.sum(jnp.where(own, column, 0.0), axis=0, keepdims=True)

    def to_column(row):
        return jnp.sum(jnp.where(own, row, 0.0), axis=1, keepdims=True)

    pick_row = lax.broadcasted_iota(jnp.int32, (width, 2 * LANES), 0)
    pick_lane = lax.broadcasted_iota(jnp.int32, (width, 2 * LANES), 1) // HALF % 2
    pick = (pick_row == pick_lane).astype(f32).astype(bf16)

    def node_sums(first, second):
        product = first * jnp.where(left_rows, first, second)
        high, low = split(product)
        return dot_transposed(pick, jnp.concatenate([high, low], axis=1))[:2]

    def inverse_factor(total):
        return 1.0 / jnp.sqrt(total[0:1] / nodes + 1e-06)


    got_cuts.wait()
    got_count.wait()
    cut = jnp.where(
        lax.broadcasted_iota(jnp.int32, (1, n_cut), 1) < count[0], cuts_ref[...], -1
    )
    for b in range(blocks):
        row = lax.broadcasted_iota(jnp.int32, (LANES, n_cut), 0) + b * LANES
        onehot[b * LANES : (b + 1) * LANES] = (row == cut).astype(f32).astype(bf16)
    got_start.wait()
    for b in range(blocks):
        set_block(K, b, start_ref[:, b * LANES : (b + 1) * LANES])
    got_prior.wait()
    for b in range(blocks):
        set_block(Q, b, prior_ref[:, b * LANES : (b + 1) * LANES])

    choose(K, 0)
    choose(Q, 0)
    pl.semaphore_wait(barrier, n_dom + n_panel - 2)

    def split_tiles(source, target):
        def step(t, _):
            high, low = split(source[t])
            target[t] = jnp.concatenate([high, low], axis=1)
            return 0

        lax.fori_loop(0, source.shape[0], step, 0)

    def advance(kind, j):
        images = boundary(kind, j)
        square = jnp.zeros((width, LANES), f32)
        cross = jnp.zeros((width, LANES), f32)
        if kind == K and j == 0:
            for b in range(blocks):
                square += field[K, b] * field[K, b]
                cross += field[K, b] * images[b]
        for b in range(blocks):
            set_block(kind, b, images[b])
        if j + 1 < ITERS - kind:
            choose(kind, j + 1)
            send_far(kind, j + 1)
        if kind == K and j == 0:
            send_sum("dom", 0, jnp.concatenate([to_row(square), to_row(cross)], axis=0))
        send_nodes(2 * (j + 1) + kind, lambda b: field[kind, b])

    f_block, f_dirs = 2 * ITERS + 1, 2 * ITERS + 2

    send_far(K, 0)
    send_nodes(0, lambda b: field[K, b])
    got_tiles.wait()
    split_tiles(tiles_ref, weights)
    send_far(Q, 0)
    send_nodes(1, lambda b: field[Q, b])
    got_btiles.wait()
    split_tiles(btiles_ref, bweights)
    for copy in got_index:
        copy.wait()
    interior((K, Q))
    advance(K, 0)
    for copy in got_rot:
        copy.wait()
    put_matrix(xp_cat, 0, rot_ref[2])
    put_matrix(pp_cat, 0, rot_ref[4])
    receive(y_data, 0, 0)
    receive(p_data, 1, 0)
    advance(Q, 0)
    interior((K, Q))
    send_sum("panel", 1, wait_sum("dom", 0))
    receive(y_data, 2, 1)
    receive(p_data, 3, 1)
    advance(K, 1)
    advance(Q, 1)

    scale, ritz = scale_matrices(0, wait_sum("panel", 1))
    receive(y_data, 4, 2)
    now = new_y(0, 0, 2)
    send_sum("panel", 2, node_sums(now[0], now[1]))
    put_y(0, 0, now)
    interior((K, Q))
    advance(K, 2)
    scale_direction_matrices(scale, ritz)
    put_p(0, 0, new_p(0, 0, 2))
    send_sum("dom", 3, wait_sum("panel", 2))
    advance(Q, 2)
    interior((K,))
    receive(p_data, 5, 2)
    receive(y_data, 6, 3)
    put_y(0, 2, new_y(0, 2, 1))
    put_p(0, 2, new_p(0, 2, 1))

    scale, ritz = scale_matrices(1, wait_sum("dom", 3))
    now = new_y(1, 0, 2)
    send_sum("panel", 4, node_sums(now[0], now[1]))
    put_y(1, 0, now)
    advance(K, 3)
    scale_direction_matrices(scale, ritz)
    put_p(1, 0, new_p(1, 0, 2))
    send_sum("dom", 5, wait_sum("panel", 4))
    receive(p_data, 7, 3)
    receive(y_data, 8, 4)
    put_y(0, 3, new_y(0, 3, 1))
    put_y(1, 2, new_y(1, 2, 1))

    scale, ritz = scale_matrices(2, wait_sum("dom", 5))
    now = new_y(2, 0, 2)
    send_sum("panel", 6, node_sums(now[0], now[1]))
    put_y(2, 0, now)
    scale_direction_matrices(scale, ritz)
    put_p(2, 0, new_p(2, 0, 1))
    send_sum("dom", 7, wait_sum("panel", 6))

    scale, ritz = scale_matrices(3, wait_sum("dom", 7))
    now = new_y(3, 0, 1)[0]
    send_sum("panel", 8, node_sums(now, now))
    pack(f_block, now)
    move(f_block)
    scale_direction_matrices(scale, ritz)
    pack(f_dirs, new_p(3, 0, 1)[0])
    move(f_dirs)
    send_sum("dom", 9, wait_sum("panel", 8))

    for slot in range(2 * ITERS - 1):
        arrive(far_in[slot].at[pl.ds(0, (n_dom - 1) * halves)], far_send.at[slot])
    for slot in range(2 * ITERS + 3):
        arrive(move_in.at[slot, pl.ds(0, n_panel - 1)], move_send.at[slot])
    for slot in range(2 * ITERS + 2):
        n = n_panel if slot in (1, 2, 4, 6, 8) else n_dom
        arrive(sum_in.at[slot, pl.ds(0, n - 1)], sum_send.at[slot])

    ritz_column = to_column(ritz + SHIFT)
    narrow = lax.broadcasted_iota(jnp.int32, (width, LANES), 1) == lax.broadcasted_iota(
        jnp.int32, (width, LANES), 0
    )
    ritz_ref[...] = jnp.sum(jnp.where(narrow, ritz_column, 0.0), axis=0, keepdims=True)

    def put_dirs(b, value):
        dirs_ref[:, b * LANES : (b + 1) * LANES] = value

    wait_move(f_dirs)
    assemble(f_dirs, put_dirs)
    wait_move(f_block)
    scale = to_column(inverse_factor(wait_sum("dom", 2 * ITERS + 1)))

    def put_block(b, value):
        block_ref[:, b * LANES : (b + 1) * LANES] = value * scale

    assemble(f_block, put_block)

def publish(block_in, dirs_in, ritz_in, block_ref, dirs_ref, ritz_ref, sems):
    block_ref[...] = block_in[...]
    dirs_ref[...] = dirs_in[...]
    ritz_ref[...] = ritz_in[:, : ritz_ref.shape[1]]


def local(n_dom, n_panel, *args):
    start, prior, degree, tiles, trows, tcols, cuts, count, btiles, brows, bcols = args[:11]
    width, ndev = start.shape
    blocks = ndev // LANES
    n_tiles, n_bound, n_cut = tiles.shape[0], btiles.shape[0], cuts.shape[0]
    rows = args[11].shape[0]
    f32, bf16, i32 = jnp.float32, jnp.bfloat16, jnp.int32
    vmem, dma = pltpu.VMEM, pltpu.SemaphoreType.DMA
    n_far, n_move, n_sum = 2 * ITERS - 1, 2 * ITERS + 3, 2 * ITERS + 2

    def smem(shape):
        return pltpu.SMEM(shape, i32)

    scratch = [
        vmem((width, ndev), f32),
        vmem((width, ndev), f32),
        vmem((1, ndev), f32),
        vmem(tiles.shape, f32),
        smem(trows.shape),
        smem(tcols.shape),
        vmem((1, n_cut), i32),
        smem(count.shape),
        vmem(btiles.shape, f32),
        smem(brows.shape),
        smem(bcols.shape),
        vmem((5, rows, rows), f32),
        dma((16,)),
        vmem((ndev, n_cut), bf16),
        vmem((n_tiles, LANES, 2 * LANES), bf16),
        vmem((n_bound, LANES, 2 * LANES), bf16),
        vmem((rows, 2 * rows), bf16),
        vmem((rows, 2 * rows), bf16),
        vmem((2, rows, 4 * rows), bf16),
        vmem((rows, 4 * rows), bf16),
        vmem((2, blocks, width, LANES), f32),
        vmem((blocks, 4 * width, 2 * LANES), bf16),
        vmem((2, blocks, width, LANES), f32),
        vmem((2, 2 * rows, (ITERS + 1) * LANES), bf16),
        vmem((2, 2 * rows, ITERS * LANES), bf16),
        vmem((n_far, n_cut // LANES, width, LANES), f32),
        (vmem((n_dom * n_cut // LANES, width, LANES), f32),) * n_far,
        vmem((n_move, n_panel, 8, LANES), f32),
        vmem((n_move, n_panel, 8, LANES), f32),
        vmem((n_sum, 2, rows), f32),
        vmem((n_sum, max(n_dom, n_panel), 2, rows), f32),
    ]
    for slots in (n_far, n_move, n_sum):
        scratch += [dma((slots,)), dma((slots,))]

    block, dirs, ritz = pl.pallas_call(
        functools.partial(kernel, ndev * n_dom),
        out_shape=(
            jax.ShapeDtypeStruct((width, ndev), f32),
            jax.ShapeDtypeStruct((width, ndev), f32),
            jax.ShapeDtypeStruct((1, LANES), f32),
        ),
        in_specs=[pl.BlockSpec(memory_space=pl.ANY)] * 16,
        out_specs=(pl.BlockSpec(memory_space=pltpu.VMEM),) * 3,
        scratch_shapes=scratch,
        compiler_params=pltpu.CompilerParams(
            collective_id=0, has_side_effects=True, vmem_limit_bytes=60 * 1024 * 1024
        ),
    )(
        start,
        prior,
        degree.reshape(1, -1),
        tiles,
        trows,
        tcols,
        cuts.reshape(1, -1),
        count,
        btiles,
        brows,
        bcols,
        *args[11:],
    )
    block, dirs, ritz = pl.pallas_call(
        publish,
        out_shape=(
            jax.ShapeDtypeStruct((width, ndev), f32),
            jax.ShapeDtypeStruct((width, ndev), f32),
            jax.ShapeDtypeStruct((1, width), f32),
        ),
        in_specs=[pl.BlockSpec(memory_space=pltpu.VMEM)] * 2
        + [pl.BlockSpec(memory_space=pltpu.VMEM)],
        out_specs=[pl.BlockSpec(memory_space=pltpu.VMEM)] * 2
        + [pl.BlockSpec(memory_space=pltpu.VMEM)],
        scratch_shapes=[dma((2,))],
    )(block, dirs, ritz)
    return block, dirs, ritz.reshape(-1)


def solution(mesh):
    return jax.shard_map(
        functools.partial(local, mesh.shape["dom"], mesh.shape["panel"]),
        mesh=mesh,
        in_specs=(
            P("panel", "dom"),
            P("panel", "dom"),
            P("dom"),
            P("dom", None, None),
            P("dom"),
            P("dom"),
            P("dom"),
            P("dom"),
            P("dom", None, None),
            P("dom"),
            P("dom"),
            P(),
            P(),
            P(),
            P(),
            P(),
        ),
        out_specs=(P("panel", "dom"), P("panel", "dom"), P("panel")),
        check_vma=False,
    )
```

```python
import functools
import math

import jax
import jax.numpy as jnp
from jax import lax
from jax.experimental import pallas as pl
from jax.experimental.pallas import tpu as pltpu
from jax.sharding import PartitionSpec as P

ITERS = 4
MESH = pl.DeviceIdType.MESH
LANES = 128
HALF = 64
UNROLL = 16
K, Q = 0, 1
SHIFT = 2.5


def split(value):
    high = value.astype(jnp.bfloat16)
    low = (value - high.astype(jnp.float32)).astype(jnp.bfloat16)
    return high, low


def swap(value):
    return pltpu.roll(value, HALF, value.ndim - 1)


def left_half(shape):
    return lax.broadcasted_iota(jnp.int32, shape, len(shape) - 1) < HALF


def dot(left, right):
    return jnp.dot(left, right, preferred_element_type=jnp.float32)


def dot_transposed(left, right):
    return lax.dot_general(
        left, right, (((1,), (1,)), ((), ())), preferred_element_type=jnp.float32
    )


def kernel(
    nodes,
    start_hbm,
    prior_hbm,
    degree_hbm,
    tiles_hbm,
    trows_hbm,
    tcols_hbm,
    cuts_hbm,
    count_hbm,
    btiles_hbm,
    brows_hbm,
    bcols_hbm,
    xx_hbm,
    xr_hbm,
    xp_hbm,
    pr_hbm,
    pp_hbm,
    block_ref,
    dirs_ref,
    ritz_ref,
    start_ref,
    prior_ref,
    degree_ref,
    tiles_ref,
    trows,
    tcols,
    cuts_ref,
    count,
    btiles_ref,
    brows,
    bcols,
    rot_ref,
    load_sem,
    onehot,
    weights,
    bweights,
    xp_cat,
    pp_cat,
    y_cat,
    p_cat,
    field,
    stacked,
    acc,
    y_data,
    p_data,
    far_out,
    far_in,
    move_out,
    move_in,
    sum_out,
    sum_in,
    far_send,
    far_recv,
    move_send,
    move_recv,
    sum_send,
    sum_recv,
):
    dom, panel = lax.axis_index("dom"), lax.axis_index("panel")
    n_dom, n_panel = lax.axis_size("dom"), lax.axis_size("panel")
    blocks, width = field.shape[1], field.shape[2]
    n_tiles, n_bound = weights.shape[0], bweights.shape[0]
    rows = rot_ref.shape[1]
    n_cut = cuts_ref.shape[1]
    halves = n_cut // LANES
    f32, bf16 = jnp.float32, jnp.bfloat16

    side = math.isqrt(n_dom)
    dom_y, dom_x = dom // side, dom % side
    panel_z, core = panel // 2, panel % 2
    dom_steps = [(y, x) for y in range(n_dom // side) for x in range(side)][1:]
    dom_steps.sort(key=lambda s: -min(s[0], n_dom // side - s[0]) - min(s[1], side - s[1]))
    panel_steps = [(z, c) for z in range(n_panel // 2) for c in range(2)][1:]
    panel_steps.sort(key=lambda s: -min(s[0], n_panel // 2 - s[0]))
    peers = {
        "dom": [
            (dom_y + y) % (n_dom // side) * side + (dom_x + x) % side for y, x in dom_steps
        ],
        "panel": [(panel_z + z) % (n_panel // 2) * 2 + (core + c) % 2 for z, c in panel_steps],
    }

    barrier = pltpu.get_barrier_semaphore()
    for axis in ("dom", "panel"):
        for peer in peers[axis]:
            pl.semaphore_signal(barrier, inc=1, device_id={axis: peer}, device_id_type=MESH)

    loads = []

    def load(src, dst):
        copy = pltpu.make_async_copy(src, dst, load_sem.at[len(loads)])
        copy.start()
        loads.append(copy)
        return copy

    got_cuts = load(cuts_hbm, cuts_ref)
    got_count = load(count_hbm, count)
    got_start = load(start_hbm, start_ref)
    got_prior = load(prior_hbm, prior_ref)
    got_index = [
        load(trows_hbm, trows),
        load(tcols_hbm, tcols),
        load(brows_hbm, brows),
        load(bcols_hbm, bcols),
        load(degree_hbm, degree_ref),
    ]
    got_tiles = load(tiles_hbm, tiles_ref)
    got_btiles = load(btiles_hbm, btiles_ref)
    got_rot = [
        load(src, rot_ref.at[at])
        for at, src in enumerate((xx_hbm, xr_hbm, xp_hbm, pr_hbm, pp_hbm))
    ]

    def spread(axis, source, target, send, recv):
        me = dom if axis == "dom" else panel
        for peer in peers[axis]:
            pltpu.make_async_remote_copy(
                src_ref=source(peer),
                dst_ref=target(me),
                send_sem=send,
                recv_sem=recv,
                device_id={axis: peer},
                device_id_type=MESH,
            ).start()

    def arrive(like, sem):
        pltpu.make_async_copy(like, like, sem).wait()


    def set_block(kind, b, value):
        field[kind, b] = value
        high, low = split(value)
        both = jnp.concatenate([high, low], axis=0)
        at = kind * 2 * width
        stacked[b, at : at + 2 * width] = jnp.concatenate([both, both], axis=1)

    def choose(kind, j):
        at = kind * 2 * width
        chosen = jnp.zeros((2 * width, n_cut), f32)
        for b in range(blocks):
            chosen += dot(
                stacked[b, at : at + 2 * width, :LANES], onehot[b * LANES : (b + 1) * LANES]
            )
        chosen = chosen[:width] + chosen[width:]
        slot = 2 * j + kind
        for h in range(halves):
            far_out[slot, h] = chosen[:, h * LANES : (h + 1) * LANES]

    def send_far(kind, j):
        slot = 2 * j + kind
        spread(
            "dom",
            lambda q: far_out.at[slot],
            lambda q: far_in[slot].at[pl.ds(q * halves, halves)],
            far_send.at[slot],
            far_recv.at[slot],
        )
        far_in[slot][pl.ds(dom * halves, halves)] = far_out[slot]

    def collect(totals, products, row_ids):
        totals = list(totals)
        for product, row in zip(products, row_ids):
            for r in range(blocks):
                totals[r] = totals[r] + jnp.where(row == r, product, 0.0)
        return tuple(totals)

    def interior(kinds):
        wide = 2 * width * len(kinds)

        def step(i, totals):
            products, row_ids = [], []
            for u in range(min(UNROLL, n_tiles)):
                t = i * min(UNROLL, n_tiles) + u
                product = dot_transposed(stacked[tcols[t], :wide], weights[t])
                parts = [
                    product[2 * width * n : 2 * width * n + width]
                    + product[2 * width * n + width : 2 * width * (n + 1)]
                    for n in range(len(kinds))
                ]
                products.append(jnp.concatenate(parts, axis=0))
                row_ids.append(trows[t])
            return collect(totals, products, row_ids)

        zero = jnp.zeros((width * len(kinds), LANES), f32)
        totals = lax.fori_loop(0, n_tiles // min(UNROLL, n_tiles), step, (zero,) * blocks)
        for b in range(blocks):
            for n in range(len(kinds)):
                acc[n, b] = totals[b][n * width : (n + 1) * width]

    def boundary(kind, j):
        slot = 2 * j + kind
        arrive(far_in[slot].at[pl.ds(0, (n_dom - 1) * halves)], far_recv.at[slot])

        def step(i, totals):
            products, row_ids = [], []
            for u in range(min(UNROLL, n_bound)):
                t = i * min(UNROLL, n_bound) + u
                high, low = split(far_in[slot][bcols[t]])
                both = jnp.concatenate([high, low], axis=0)
                product = dot_transposed(jnp.concatenate([both, both], axis=1), bweights[t])
                products.append(product[:width] + product[width:])
                row_ids.append(brows[t])
            return collect(totals, products, row_ids)

        totals = lax.fori_loop(
            0,
            n_bound // min(UNROLL, n_bound),
            step,
            tuple(acc[kind, b] for b in range(blocks)),
        )
        return [
            (degree_ref[:, b * LANES : (b + 1) * LANES] - SHIFT) * field[kind, b] - totals[b]
            for b in range(blocks)
        ]

    left8 = left_half((8, LANES))

    def send_nodes(slot, values):
        for b in range(blocks):
            value = values(b)
            top, bottom = value[:8], value[8:]
            move_out[slot, 2 * b] = jnp.where(left8, top, swap(bottom))
            move_out[slot, 2 * b + 1] = jnp.where(left8, swap(top), bottom)
        move(slot)

    def move(slot):
        spread(
            "panel",
            lambda q: move_out.at[slot, q],
            lambda q: move_in.at[slot, q],
            move_send.at[slot],
            move_recv.at[slot],
        )
        move_in[slot, panel] = move_out[slot, panel]

    def wait_move(slot):
        arrive(move_in.at[slot, pl.ds(0, n_panel - 1)], move_recv.at[slot])

    def assemble(slot, put):
        for b in range(blocks):
            first, second = move_in[slot, 2 * b], move_in[slot, 2 * b + 1]
            top = jnp.where(left8, first, swap(second))
            bottom = jnp.where(left8, swap(first), second)
            put(b, jnp.concatenate([top, bottom], axis=0))


    def unpack(slot):
        got = move_in[slot]
        turned = swap(got)
        left = left_half(got.shape)
        top = jnp.where(left, got, turned)
        bottom = jnp.where(left, turned, got)
        return jnp.concatenate([top[:, None], bottom[:, None]], axis=1).reshape(rows, LANES)

    left_rows = left_half((rows, LANES))

    def put_operand(data, at, j, value):
        high = value.astype(bf16).astype(f32)
        lanes = slice(j * LANES, (j + 1) * LANES)
        data[at, :rows, lanes] = jnp.where(left_rows, high, value - high).astype(bf16)
        data[at, rows:, lanes] = jnp.where(left_rows, high, 0.0).astype(bf16)

    def receive(data, slot, j):
        wait_move(slot)
        put_operand(data, 0, j, unpack(slot))

    def put_matrix(ref, at, matrix):
        high, low = split(matrix)
        ref[:, at * 2 * rows : at * 2 * rows + rows] = high
        ref[:, at * 2 * rows + rows : (at + 1) * 2 * rows] = low

    def scale_matrices(k, total):
        scale = inverse_factor(total)
        ritz = total[1:2] / total[0:1]
        xr_scaled = rot_ref[1] * scale
        put_matrix(y_cat.at[k % 2], 0, rot_ref[0] * scale - xr_scaled * ritz)
        put_matrix(y_cat.at[k % 2], 1, xr_scaled)
        return scale, ritz

    def scale_direction_matrices(scale, ritz):
        pr_scaled = rot_ref[3] * scale
        put_matrix(p_cat, 0, -pr_scaled * ritz)
        put_matrix(p_cat, 1, pr_scaled)

    def new_y(k, first, count, base=None):
        return rotate(y_cat.at[k % 2], xp_cat, k, first, count, base)

    def new_p(k, first, count):
        return rotate(p_cat, pp_cat, k, first, count)

    def put_y(k, first, values):
        for n, value in enumerate(values):
            put_operand(y_data, (k + 1) % 2, first + n, value)

    def put_p(k, first, values):
        for n, value in enumerate(values):
            put_operand(p_data, (k + 1) % 2, first + n, value)

    def from_directions(from_cat, k, first, count):
        return dot(from_cat[...], p_data[k % 2, :, first * LANES : (first + count) * LANES])

    def rotate(matrices, from_cat, k, first, count, base=None):
        now = k % 2
        lo, hi = first * LANES, (first + count) * LANES
        total = from_directions(from_cat, k, first, count) if base is None else base
        total += dot(matrices[:, : 2 * rows], y_data[now, :, lo:hi])
        total += dot(matrices[:, 2 * rows :], y_data[now, :, lo + LANES : hi + LANES])
        values = []
        for n in range(count):
            part = total[:, n * LANES : (n + 1) * LANES]
            values.append(part + swap(part))
        return values

    def pack(slot, value):
        value4 = value.reshape(n_panel, 2, 8, LANES)
        move_out[slot] = jnp.where(
            left_half((n_panel, 8, LANES)), value4[:, 0], value4[:, 1]
        )


    def send_sum(axis, slot, value):
        sum_out[slot] = value
        spread(
            axis,
            lambda q: sum_out.at[slot],
            lambda q: sum_in.at[slot, q],
            sum_send.at[slot],
            sum_recv.at[slot],
        )
        sum_in[slot, dom if axis == "dom" else panel] = value

    def wait_sum(axis, slot):
        n = n_dom if axis == "dom" else n_panel
        arrive(sum_in.at[slot, pl.ds(0, n - 1)], sum_recv.at[slot])
        return jnp.sum(sum_in[slot, :n], axis=0)

    own = lax.broadcasted_iota(jnp.int32, (width, rows), 1) == (
        lax.broadcasted_iota(jnp.int32, (width, rows), 0) + panel * width
    )

    def to_row(partial):
        column = jnp.sum(partial, axis=1, keepdims=True)
        return jnp.sum(jnp.where(own, column, 0.0), axis=0, keepdims=True)

    def to_column(row):
        return jnp.sum(jnp.where(own, row, 0.0), axis=1, keepdims=True)

    pick_row = lax.broadcasted_iota(jnp.int32, (width, 2 * LANES), 0)
    pick_lane = lax.broadcasted_iota(jnp.int32, (width, 2 * LANES), 1) // HALF % 2
    pick = (pick_row == pick_lane).astype(f32).astype(bf16)

    def node_sums(first, second):
        product = first * jnp.where(left_rows, first, second)
        high, low = split(product)
        return dot_transposed(pick, jnp.concatenate([high, low], axis=1))[:2]

    def inverse_factor(total):
        return 1.0 / jnp.sqrt(total[0:1] / nodes + 1e-06)


    got_cuts.wait()
    got_count.wait()
    cut = jnp.where(
        lax.broadcasted_iota(jnp.int32, (1, n_cut), 1) < count[0], cuts_ref[...], -1
    )
    for b in range(blocks):
        row = lax.broadcasted_iota(jnp.int32, (LANES, n_cut), 0) + b * LANES
        onehot[b * LANES : (b + 1) * LANES] = (row == cut).astype(f32).astype(bf16)
    got_start.wait()
    for b in range(blocks):
        set_block(K, b, start_ref[:, b * LANES : (b + 1) * LANES])
    got_prior.wait()
    for b in range(blocks):
        set_block(Q, b, prior_ref[:, b * LANES : (b + 1) * LANES])

    choose(K, 0)
    choose(Q, 0)
    pl.semaphore_wait(barrier, n_dom + n_panel - 2)

    def split_tiles(source, target):
        def step(t, _):
            high, low = split(source[t])
            target[t] = jnp.concatenate([high, low], axis=1)
            return 0

        lax.fori_loop(0, source.shape[0], step, 0)

    def advance(kind, j):
        images = boundary(kind, j)
        if j > 0:
            send_nodes(2 * (j + 1) + kind, lambda b: images[b])
        if kind == K and j == 0:
            square = jnp.zeros((width, LANES), f32)
            cross = jnp.zeros((width, LANES), f32)
            for b in range(blocks):
                square += field[K, b] * field[K, b]
                cross += field[K, b] * images[b]
            send_sum("dom", 0, jnp.concatenate([to_row(square), to_row(cross)], axis=0))
        for b in range(blocks):
            set_block(kind, b, images[b])
        if j + 1 < ITERS - kind:
            choose(kind, j + 1)
            send_far(kind, j + 1)
        if j == 0:
            send_nodes(2 * (j + 1) + kind, lambda b: images[b])

    f_block, f_dirs = 2 * ITERS + 1, 2 * ITERS + 2

    send_far(K, 0)
    send_nodes(0, lambda b: field[K, b])
    got_tiles.wait()
    split_tiles(tiles_ref, weights)
    send_far(Q, 0)
    send_nodes(1, lambda b: field[Q, b])
    got_btiles.wait()
    split_tiles(btiles_ref, bweights)
    for copy in got_index:
        copy.wait()
    interior((K, Q))
    advance(K, 0)
    for copy in got_rot:
        copy.wait()
    put_matrix(xp_cat, 0, rot_ref[2])
    put_matrix(pp_cat, 0, rot_ref[4])
    receive(y_data, 0, 0)
    receive(p_data, 1, 0)
    advance(Q, 0)
    interior((K, Q))
    send_sum("panel", 1, wait_sum("dom", 0))
    advance(K, 1)
    receive(y_data, 2, 1)
    receive(p_data, 3, 1)
    advance(Q, 1)

    base = from_directions(xp_cat, 0, 0, 2)
    scale, ritz = scale_matrices(0, wait_sum("panel", 1))
    base += dot(y_cat[0, :, : 2 * rows], y_data[0, :, : 2 * LANES])
    near = base[:, :LANES] + dot(y_cat[0, :, 2 * rows :], y_data[0, :, LANES : 2 * LANES])
    receive(y_data, 4, 2)
    next_ = base[:, LANES:] + dot(y_cat[0, :, 2 * rows :], y_data[0, :, 2 * LANES : 3 * LANES])
    now = [near + swap(near), next_ + swap(next_)]
    send_sum("panel", 2, node_sums(now[0], now[1]))
    put_y(0, 0, now)
    interior((K, Q))
    advance(K, 2)
    scale_direction_matrices(scale, ritz)
    put_p(0, 0, new_p(0, 0, 2))
    send_sum("dom", 3, wait_sum("panel", 2))
    advance(Q, 2)
    interior((K,))
    receive(p_data, 5, 2)
    receive(y_data, 6, 3)
    put_y(0, 2, new_y(0, 2, 1))
    put_p(0, 2, new_p(0, 2, 1))

    base = from_directions(xp_cat, 1, 0, 2)
    scale, ritz = scale_matrices(1, wait_sum("dom", 3))
    now = new_y(1, 0, 2, base)
    send_sum("panel", 4, node_sums(now[0], now[1]))
    put_y(1, 0, now)
    advance(K, 3)
    scale_direction_matrices(scale, ritz)
    put_p(1, 0, new_p(1, 0, 2))
    send_sum("dom", 5, wait_sum("panel", 4))
    receive(p_data, 7, 3)
    receive(y_data, 8, 4)
    put_y(0, 3, new_y(0, 3, 1))
    put_y(1, 2, new_y(1, 2, 1))

    base = from_directions(xp_cat, 2, 0, 2)
    scale, ritz = scale_matrices(2, wait_sum("dom", 5))
    now = new_y(2, 0, 2, base)
    send_sum("panel", 6, node_sums(now[0], now[1]))
    put_y(2, 0, now)
    scale_direction_matrices(scale, ritz)
    put_p(2, 0, new_p(2, 0, 1))
    send_sum("dom", 7, wait_sum("panel", 6))

    base = from_directions(xp_cat, 3, 0, 1)
    scale, ritz = scale_matrices(3, wait_sum("dom", 7))
    now = new_y(3, 0, 1, base)[0]
    send_sum("panel", 8, node_sums(now, now))
    pack(f_block, now)
    move(f_block)
    scale_direction_matrices(scale, ritz)
    pack(f_dirs, new_p(3, 0, 1)[0])
    move(f_dirs)
    send_sum("dom", 9, wait_sum("panel", 8))

    for slot in range(2 * ITERS - 1):
        arrive(far_in[slot].at[pl.ds(0, (n_dom - 1) * halves)], far_send.at[slot])
    for slot in range(2 * ITERS + 3):
        arrive(move_in.at[slot, pl.ds(0, n_panel - 1)], move_send.at[slot])
    for slot in range(2 * ITERS + 2):
        n = n_panel if slot in (1, 2, 4, 6, 8) else n_dom
        arrive(sum_in.at[slot, pl.ds(0, n - 1)], sum_send.at[slot])

    ritz_column = to_column(ritz + SHIFT)
    narrow = lax.broadcasted_iota(jnp.int32, (width, LANES), 1) == lax.broadcasted_iota(
        jnp.int32, (width, LANES), 0
    )
    ritz_ref[...] = jnp.sum(jnp.where(narrow, ritz_column, 0.0), axis=0, keepdims=True)

    def put_dirs(b, value):
        dirs_ref[:, b * LANES : (b + 1) * LANES] = value

    wait_move(f_dirs)
    assemble(f_dirs, put_dirs)
    wait_move(f_block)
    scale = to_column(inverse_factor(wait_sum("dom", 2 * ITERS + 1)))

    def put_block(b, value):
        block_ref[:, b * LANES : (b + 1) * LANES] = value * scale

    assemble(f_block, put_block)

def publish(block_in, dirs_in, ritz_in, block_ref, dirs_ref, ritz_ref, sems):
    block_ref[...] = block_in[...]
    dirs_ref[...] = dirs_in[...]
    ritz_ref[...] = ritz_in[:, : ritz_ref.shape[1]]


def local(n_dom, n_panel, *args):
    start, prior, degree, tiles, trows, tcols, cuts, count, btiles, brows, bcols = args[:11]
    width, ndev = start.shape
    blocks = ndev // LANES
    n_tiles, n_bound, n_cut = tiles.shape[0], btiles.shape[0], cuts.shape[0]
    rows = args[11].shape[0]
    f32, bf16, i32 = jnp.float32, jnp.bfloat16, jnp.int32
    vmem, dma = pltpu.VMEM, pltpu.SemaphoreType.DMA
    n_far, n_move, n_sum = 2 * ITERS - 1, 2 * ITERS + 3, 2 * ITERS + 2

    def smem(shape):
        return pltpu.SMEM(shape, i32)

    scratch = [
        vmem((width, ndev), f32),
        vmem((width, ndev), f32),
        vmem((1, ndev), f32),
        vmem(tiles.shape, f32),
        smem(trows.shape),
        smem(tcols.shape),
        vmem((1, n_cut), i32),
        smem(count.shape),
        vmem(btiles.shape, f32),
        smem(brows.shape),
        smem(bcols.shape),
        vmem((5, rows, rows), f32),
        dma((16,)),
        vmem((ndev, n_cut), bf16),
        vmem((n_tiles, LANES, 2 * LANES), bf16),
        vmem((n_bound, LANES, 2 * LANES), bf16),
        vmem((rows, 2 * rows), bf16),
        vmem((rows, 2 * rows), bf16),
        vmem((2, rows, 4 * rows), bf16),
        vmem((rows, 4 * rows), bf16),
        vmem((2, blocks, width, LANES), f32),
        vmem((blocks, 4 * width, 2 * LANES), bf16),
        vmem((2, blocks, width, LANES), f32),
        vmem((2, 2 * rows, (ITERS + 1) * LANES), bf16),
        vmem((2, 2 * rows, ITERS * LANES), bf16),
        vmem((n_far, n_cut // LANES, width, LANES), f32),
        (vmem((n_dom * n_cut // LANES, width, LANES), f32),) * n_far,
        vmem((n_move, n_panel, 8, LANES), f32),
        vmem((n_move, n_panel, 8, LANES), f32),
        vmem((n_sum, 2, rows), f32),
        vmem((n_sum, max(n_dom, n_panel), 2, rows), f32),
    ]
    for slots in (n_far, n_move, n_sum):
        scratch += [dma((slots,)), dma((slots,))]

    block, dirs, ritz = pl.pallas_call(
        functools.partial(kernel, ndev * n_dom),
        out_shape=(
            jax.ShapeDtypeStruct((width, ndev), f32),
            jax.ShapeDtypeStruct((width, ndev), f32),
            jax.ShapeDtypeStruct((1, LANES), f32),
        ),
        in_specs=[pl.BlockSpec(memory_space=pl.ANY)] * 16,
        out_specs=(pl.BlockSpec(memory_space=pltpu.VMEM),) * 3,
        scratch_shapes=scratch,
        compiler_params=pltpu.CompilerParams(
            collective_id=0, has_side_effects=True, vmem_limit_bytes=60 * 1024 * 1024
        ),
    )(
        start,
        prior,
        degree.reshape(1, -1),
        tiles,
        trows,
        tcols,
        cuts.reshape(1, -1),
        count,
        btiles,
        brows,
        bcols,
        *args[11:],
    )
    block, dirs, ritz = pl.pallas_call(
        publish,
        out_shape=(
            jax.ShapeDtypeStruct((width, ndev), f32),
            jax.ShapeDtypeStruct((width, ndev), f32),
            jax.ShapeDtypeStruct((1, width), f32),
        ),
        in_specs=[pl.BlockSpec(memory_space=pltpu.VMEM)] * 2
        + [pl.BlockSpec(memory_space=pltpu.VMEM)],
        out_specs=[pl.BlockSpec(memory_space=pltpu.VMEM)] * 2
        + [pl.BlockSpec(memory_space=pltpu.VMEM)],
        scratch_shapes=[dma((2,))],
    )(block, dirs, ritz)
    return block, dirs, ritz.reshape(-1)


def solution(mesh):
    return jax.shard_map(
        functools.partial(local, mesh.shape["dom"], mesh.shape["panel"]),
        mesh=mesh,
        in_specs=(
            P("panel", "dom"),
            P("panel", "dom"),
            P("dom"),
            P("dom", None, None),
            P("dom"),
            P("dom"),
            P("dom"),
            P("dom"),
            P("dom", None, None),
            P("dom"),
            P("dom"),
            P(),
            P(),
            P(),
            P(),
            P(),
        ),
        out_specs=(P("panel", "dom"), P("panel", "dom"), P("panel")),
        check_vma=False,
    )
```

```python
import functools
import math

import jax
import jax.numpy as jnp
from jax import lax
from jax.experimental import pallas as pl
from jax.experimental.pallas import tpu as pltpu
from jax.sharding import PartitionSpec as P

ITERS = 4
MESH = pl.DeviceIdType.MESH
LANES = 128
HALF = 64
UNROLL = 16
K, Q = 0, 1
SHIFT = 2.5


def split(value):
    high = value.astype(jnp.bfloat16)
    low = (value - high.astype(jnp.float32)).astype(jnp.bfloat16)
    return high, low


def swap(value):
    return pltpu.roll(value, HALF, value.ndim - 1)


def left_half(shape):
    return lax.broadcasted_iota(jnp.int32, shape, len(shape) - 1) < HALF


def dot(left, right):
    return jnp.dot(left, right, preferred_element_type=jnp.float32)


def dot_transposed(left, right):
    return lax.dot_general(
        left, right, (((1,), (1,)), ((), ())), preferred_element_type=jnp.float32
    )


def kernel(
    nodes,
    start_hbm,
    prior_hbm,
    degree_hbm,
    tiles_hbm,
    trows_hbm,
    tcols_hbm,
    cuts_hbm,
    count_hbm,
    btiles_hbm,
    brows_hbm,
    bcols_hbm,
    xx_hbm,
    xr_hbm,
    xp_hbm,
    pr_hbm,
    pp_hbm,
    block_ref,
    dirs_ref,
    ritz_ref,
    start_ref,
    prior_ref,
    degree_ref,
    tiles_ref,
    trows,
    tcols,
    cuts_ref,
    count,
    btiles_ref,
    brows,
    bcols,
    rot_ref,
    load_sem,
    onehot,
    weights,
    bweights,
    xp_cat,
    pp_cat,
    y_cat,
    p_cat,
    field,
    stacked,
    acc,
    y_data,
    p_data,
    far_out,
    far_in,
    move_out,
    move_in,
    sum_out,
    sum_in,
    far_send,
    far_recv,
    move_send,
    move_recv,
    sum_send,
    sum_recv,
):
    dom, panel = lax.axis_index("dom"), lax.axis_index("panel")
    n_dom, n_panel = lax.axis_size("dom"), lax.axis_size("panel")
    blocks, width = field.shape[1], field.shape[2]
    n_tiles, n_bound = weights.shape[0], bweights.shape[0]
    rows = rot_ref.shape[1]
    n_cut = cuts_ref.shape[1]
    halves = n_cut // LANES
    f32, bf16 = jnp.float32, jnp.bfloat16

    side = math.isqrt(n_dom)
    dom_y, dom_x = dom // side, dom % side
    panel_z, core = panel // 2, panel % 2
    dom_steps = [(y, x) for y in range(n_dom // side) for x in range(side)][1:]
    dom_steps.sort(key=lambda s: -min(s[0], n_dom // side - s[0]) - min(s[1], side - s[1]))
    panel_steps = [(z, c) for z in range(n_panel // 2) for c in range(2)][1:]
    panel_steps.sort(key=lambda s: -min(s[0], n_panel // 2 - s[0]))
    peers = {
        "dom": [
            (dom_y + y) % (n_dom // side) * side + (dom_x + x) % side for y, x in dom_steps
        ],
        "panel": [(panel_z + z) % (n_panel // 2) * 2 + (core + c) % 2 for z, c in panel_steps],
    }

    barrier = pltpu.get_barrier_semaphore()
    for axis in ("dom", "panel"):
        for peer in peers[axis]:
            pl.semaphore_signal(barrier, inc=1, device_id={axis: peer}, device_id_type=MESH)

    loads = []

    def load(src, dst):
        copy = pltpu.make_async_copy(src, dst, load_sem.at[len(loads)])
        copy.start()
        loads.append(copy)
        return copy

    got_cuts = load(cuts_hbm, cuts_ref)
    got_count = load(count_hbm, count)
    got_start = load(start_hbm, start_ref)
    got_prior = load(prior_hbm, prior_ref)
    got_index = [
        load(trows_hbm, trows),
        load(tcols_hbm, tcols),
        load(brows_hbm, brows),
        load(bcols_hbm, bcols),
        load(degree_hbm, degree_ref),
    ]
    got_tiles = load(tiles_hbm, tiles_ref)
    got_btiles = load(btiles_hbm, btiles_ref)
    got_rot = [
        load(src, rot_ref.at[at])
        for at, src in enumerate((xx_hbm, xr_hbm, xp_hbm, pr_hbm, pp_hbm))
    ]

    def spread(axis, source, target, send, recv):
        me = dom if axis == "dom" else panel
        for peer in peers[axis]:
            pltpu.make_async_remote_copy(
                src_ref=source(peer),
                dst_ref=target(me),
                send_sem=send,
                recv_sem=recv,
                device_id={axis: peer},
                device_id_type=MESH,
            ).start()

    def arrive(like, sem):
        pltpu.make_async_copy(like, like, sem).wait()


    def set_block(kind, b, value):
        field[kind, b] = value
        high, low = split(value)
        both = jnp.concatenate([high, low], axis=0)
        at = kind * 2 * width
        stacked[b, at : at + 2 * width] = jnp.concatenate([both, both], axis=1)

    def choose(kind, j):
        at = kind * 2 * width
        chosen = jnp.zeros((2 * width, n_cut), f32)
        for b in range(blocks):
            chosen += dot(
                stacked[b, at : at + 2 * width, :LANES], onehot[b * LANES : (b + 1) * LANES]
            )
        chosen = chosen[:width] + chosen[width:]
        slot = 2 * j + kind
        for h in range(halves):
            far_out[slot, h] = chosen[:, h * LANES : (h + 1) * LANES]

    def send_far(kind, j):
        slot = 2 * j + kind
        spread(
            "dom",
            lambda q: far_out.at[slot],
            lambda q: far_in[slot].at[pl.ds(q * halves, halves)],
            far_send.at[slot],
            far_recv.at[slot],
        )
        far_in[slot][pl.ds(dom * halves, halves)] = far_out[slot]

    def collect(totals, products, row_ids):
        totals = list(totals)
        for product, row in zip(products, row_ids):
            for r in range(blocks):
                totals[r] = totals[r] + jnp.where(row == r, product, 0.0)
        return tuple(totals)

    def interior(kinds):
        wide = 2 * width * len(kinds)

        def step(i, totals):
            products, row_ids = [], []
            for u in range(min(UNROLL, n_tiles)):
                t = i * min(UNROLL, n_tiles) + u
                product = dot_transposed(stacked[tcols[t], :wide], weights[t])
                parts = [
                    product[2 * width * n : 2 * width * n + width]
                    + product[2 * width * n + width : 2 * width * (n + 1)]
                    for n in range(len(kinds))
                ]
                products.append(jnp.concatenate(parts, axis=0))
                row_ids.append(trows[t])
            return collect(totals, products, row_ids)

        zero = jnp.zeros((width * len(kinds), LANES), f32)
        totals = lax.fori_loop(0, n_tiles // min(UNROLL, n_tiles), step, (zero,) * blocks)
        for b in range(blocks):
            for n in range(len(kinds)):
                acc[n, b] = totals[b][n * width : (n + 1) * width]

    def boundary(kind, j):
        slot = 2 * j + kind
        arrive(far_in[slot].at[pl.ds(0, (n_dom - 1) * halves)], far_recv.at[slot])

        def step(i, totals):
            products, row_ids = [], []
            for u in range(min(UNROLL, n_bound)):
                t = i * min(UNROLL, n_bound) + u
                high, low = split(far_in[slot][bcols[t]])
                both = jnp.concatenate([high, low], axis=0)
                product = dot(jnp.concatenate([both, both], axis=1), bweights[t])
                products.append(product[:width] + product[width:])
                row_ids.append(brows[t])
            return collect(totals, products, row_ids)

        totals = lax.fori_loop(
            0,
            n_bound // min(UNROLL, n_bound),
            step,
            tuple(acc[kind, b] for b in range(blocks)),
        )
        return [
            (degree_ref[:, b * LANES : (b + 1) * LANES] - SHIFT) * field[kind, b] - totals[b]
            for b in range(blocks)
        ]

    left8 = left_half((8, LANES))

    def send_nodes(slot, values):
        for b in range(blocks):
            value = values(b)
            top, bottom = value[:8], value[8:]
            move_out[slot, 2 * b] = jnp.where(left8, top, swap(bottom))
            move_out[slot, 2 * b + 1] = jnp.where(left8, swap(top), bottom)
        move(slot)

    def move(slot):
        spread(
            "panel",
            lambda q: move_out.at[slot, q],
            lambda q: move_in.at[slot, q],
            move_send.at[slot],
            move_recv.at[slot],
        )
        move_in[slot, panel] = move_out[slot, panel]

    def wait_move(slot):
        arrive(move_in.at[slot, pl.ds(0, n_panel - 1)], move_recv.at[slot])

    def assemble(slot, put):
        for b in range(blocks):
            first, second = move_in[slot, 2 * b], move_in[slot, 2 * b + 1]
            top = jnp.where(left8, first, swap(second))
            bottom = jnp.where(left8, swap(first), second)
            put(b, jnp.concatenate([top, bottom], axis=0))


    def unpack(slot):
        got = move_in[slot]
        turned = swap(got)
        left = left_half(got.shape)
        top = jnp.where(left, got, turned)
        bottom = jnp.where(left, turned, got)
        return jnp.concatenate([top[:, None], bottom[:, None]], axis=1).reshape(rows, LANES)

    left_rows = left_half((rows, LANES))

    def put_operand(data, at, j, value):
        high = value.astype(bf16).astype(f32)
        lanes = slice(j * LANES, (j + 1) * LANES)
        data[at, :rows, lanes] = jnp.where(left_rows, high, value - high).astype(bf16)
        data[at, rows:, lanes] = jnp.where(left_rows, high, 0.0).astype(bf16)

    def receive(data, slot, j):
        wait_move(slot)
        put_operand(data, 0, j, unpack(slot))

    def put_matrix(ref, at, matrix):
        high, low = split(matrix)
        ref[:, at * 2 * rows : at * 2 * rows + rows] = high
        ref[:, at * 2 * rows + rows : (at + 1) * 2 * rows] = low

    def scale_matrices(k, total):
        scale = inverse_factor(total)
        ritz = total[1:2] / total[0:1]
        xr_scaled = rot_ref[1] * scale
        put_matrix(y_cat.at[k % 2], 0, rot_ref[0] * scale - xr_scaled * ritz)
        put_matrix(y_cat.at[k % 2], 1, xr_scaled)
        return scale, ritz

    def scale_direction_matrices(scale, ritz):
        pr_scaled = rot_ref[3] * scale
        put_matrix(p_cat, 0, -pr_scaled * ritz)
        put_matrix(p_cat, 1, pr_scaled)

    def new_y(k, first, count, base=None):
        return rotate(y_cat.at[k % 2], xp_cat, k, first, count, base)

    def new_p(k, first, count):
        return rotate(p_cat, pp_cat, k, first, count)

    def put_y(k, first, values):
        for n, value in enumerate(values):
            put_operand(y_data, (k + 1) % 2, first + n, value)

    def put_p(k, first, values):
        for n, value in enumerate(values):
            put_operand(p_data, (k + 1) % 2, first + n, value)

    def from_directions(from_cat, k, first, count):
        return dot(from_cat[...], p_data[k % 2, :, first * LANES : (first + count) * LANES])

    def rotate(matrices, from_cat, k, first, count, base=None):
        now = k % 2
        lo, hi = first * LANES, (first + count) * LANES
        total = from_directions(from_cat, k, first, count) if base is None else base
        total += dot(matrices[:, : 2 * rows], y_data[now, :, lo:hi])
        total += dot(matrices[:, 2 * rows :], y_data[now, :, lo + LANES : hi + LANES])
        values = []
        for n in range(count):
            part = total[:, n * LANES : (n + 1) * LANES]
            values.append(part + swap(part))
        return values

    def pack(slot, value):
        value4 = value.reshape(n_panel, 2, 8, LANES)
        move_out[slot] = jnp.where(
            left_half((n_panel, 8, LANES)), value4[:, 0], value4[:, 1]
        )


    def send_sum(axis, slot, value):
        sum_out[slot] = value
        spread(
            axis,
            lambda q: sum_out.at[slot],
            lambda q: sum_in.at[slot, q],
            sum_send.at[slot],
            sum_recv.at[slot],
        )
        sum_in[slot, dom if axis == "dom" else panel] = value

    def wait_sum(axis, slot):
        n = n_dom if axis == "dom" else n_panel
        arrive(sum_in.at[slot, pl.ds(0, n - 1)], sum_recv.at[slot])
        return jnp.sum(sum_in[slot, :n], axis=0)

    own = lax.broadcasted_iota(jnp.int32, (width, rows), 1) == (
        lax.broadcasted_iota(jnp.int32, (width, rows), 0) + panel * width
    )

    def to_row(partial):
        column = jnp.sum(partial, axis=1, keepdims=True)
        return jnp.sum(jnp.where(own, column, 0.0), axis=0, keepdims=True)

    def to_column(row):
        return jnp.sum(jnp.where(own, row, 0.0), axis=1, keepdims=True)

    pick_row = lax.broadcasted_iota(jnp.int32, (width, 2 * LANES), 0)
    pick_lane = lax.broadcasted_iota(jnp.int32, (width, 2 * LANES), 1) // HALF % 2
    pick = (pick_row == pick_lane).astype(f32).astype(bf16)

    def node_sums(first, second):
        product = first * jnp.where(left_rows, first, second)
        high, low = split(product)
        return dot_transposed(pick, jnp.concatenate([high, low], axis=1))[:2]

    def inverse_factor(total):
        return 1.0 / jnp.sqrt(total[0:1] / nodes + 1e-06)


    got_cuts.wait()
    got_count.wait()
    cut = jnp.where(
        lax.broadcasted_iota(jnp.int32, (1, n_cut), 1) < count[...], cuts_ref[...], -1
    )
    for b in range(blocks):
        row = lax.broadcasted_iota(jnp.int32, (LANES, n_cut), 0) + b * LANES
        onehot[b * LANES : (b + 1) * LANES] = (row == cut).astype(f32).astype(bf16)
    got_start.wait()
    for b in range(blocks):
        set_block(K, b, start_ref[:, b * LANES : (b + 1) * LANES])
    got_prior.wait()
    for b in range(blocks):
        set_block(Q, b, prior_ref[:, b * LANES : (b + 1) * LANES])

    choose(K, 0)
    choose(Q, 0)
    pl.semaphore_wait(barrier, n_dom + n_panel - 2)

    def split_turned(source, target):
        def step(t, _):
            high, low = split(source[t].T)
            target[t] = jnp.concatenate([high, low], axis=0)
            return 0

        lax.fori_loop(0, source.shape[0], step, 0)

    def split_tiles(source, target):
        def step(t, _):
            high, low = split(source[t])
            target[t] = jnp.concatenate([high, low], axis=1)
            return 0

        lax.fori_loop(0, source.shape[0], step, 0)

    def advance(kind, j):
        images = boundary(kind, j)
        if j > 0:
            send_nodes(2 * (j + 1) + kind, lambda b: images[b])
        if kind == K and j == 0:
            cross = jnp.zeros((width, LANES), f32)
            for b in range(blocks):
                cross += field[K, b] * images[b]
            send_sum("dom", 0, jnp.concatenate([square_row, to_row(cross)], axis=0))
        for b in range(blocks):
            set_block(kind, b, images[b])
        if j + 1 < ITERS - kind:
            choose(kind, j + 1)
            send_far(kind, j + 1)
        if j == 0:
            send_nodes(2 * (j + 1) + kind, lambda b: images[b])

    f_block, f_dirs = 2 * ITERS + 1, 2 * ITERS + 2

    send_far(K, 0)
    got_tiles.wait()
    split_tiles(tiles_ref, weights)
    send_far(Q, 0)
    got_btiles.wait()
    split_turned(btiles_ref, bweights)
    for copy in got_index:
        copy.wait()
    interior((K, Q))
    send_nodes(0, lambda b: field[K, b])
    send_nodes(1, lambda b: field[Q, b])
    square = jnp.zeros((width, LANES), f32)
    for b in range(blocks):
        square += field[K, b] * field[K, b]
    square_row = to_row(square)
    advance(K, 0)
    advance(Q, 0)
    interior((K, Q))
    send_sum("panel", 1, wait_sum("dom", 0))
    advance(K, 1)
    for copy in got_rot:
        copy.wait()
    put_matrix(xp_cat, 0, rot_ref[2])
    put_matrix(pp_cat, 0, rot_ref[4])
    receive(y_data, 0, 0)
    receive(p_data, 1, 0)
    receive(y_data, 2, 1)
    receive(p_data, 3, 1)
    advance(Q, 1)

    base = from_directions(xp_cat, 0, 0, 2)
    scale, ritz = scale_matrices(0, wait_sum("panel", 1))
    base += dot(y_cat[0, :, : 2 * rows], y_data[0, :, : 2 * LANES])
    near = base[:, :LANES] + dot(y_cat[0, :, 2 * rows :], y_data[0, :, LANES : 2 * LANES])
    receive(y_data, 4, 2)
    next_ = base[:, LANES:] + dot(y_cat[0, :, 2 * rows :], y_data[0, :, 2 * LANES : 3 * LANES])
    now = [near + swap(near), next_ + swap(next_)]
    send_sum("panel", 2, node_sums(now[0], now[1]))
    put_y(0, 0, now)
    interior((K, Q))
    advance(K, 2)
    scale_direction_matrices(scale, ritz)
    put_p(0, 0, new_p(0, 0, 2))
    send_sum("dom", 3, wait_sum("panel", 2))
    advance(Q, 2)
    interior((K,))
    receive(p_data, 5, 2)
    receive(y_data, 6, 3)
    put_y(0, 2, new_y(0, 2, 1))
    put_p(0, 2, new_p(0, 2, 1))

    base = from_directions(xp_cat, 1, 0, 2)
    scale, ritz = scale_matrices(1, wait_sum("dom", 3))
    now = new_y(1, 0, 2, base)
    send_sum("panel", 4, node_sums(now[0], now[1]))
    put_y(1, 0, now)
    advance(K, 3)
    scale_direction_matrices(scale, ritz)
    put_p(1, 0, new_p(1, 0, 2))
    send_sum("dom", 5, wait_sum("panel", 4))
    receive(p_data, 7, 3)
    receive(y_data, 8, 4)
    put_y(0, 3, new_y(0, 3, 1))
    put_y(1, 2, new_y(1, 2, 1))

    base = from_directions(xp_cat, 2, 0, 2)
    scale, ritz = scale_matrices(2, wait_sum("dom", 5))
    now = new_y(2, 0, 2, base)
    send_sum("panel", 6, node_sums(now[0], now[1]))
    put_y(2, 0, now)
    scale_direction_matrices(scale, ritz)
    put_p(2, 0, new_p(2, 0, 1))
    send_sum("dom", 7, wait_sum("panel", 6))

    base = from_directions(xp_cat, 3, 0, 1)
    scale, ritz = scale_matrices(3, wait_sum("dom", 7))
    now = new_y(3, 0, 1, base)[0]
    send_sum("panel", 8, node_sums(now, now))
    pack(f_block, now)
    move(f_block)
    scale_direction_matrices(scale, ritz)
    pack(f_dirs, new_p(3, 0, 1)[0])
    move(f_dirs)
    send_sum("dom", 9, wait_sum("panel", 8))

    for slot in range(2 * ITERS - 1):
        arrive(far_in[slot].at[pl.ds(0, (n_dom - 1) * halves)], far_send.at[slot])
    for slot in range(2 * ITERS + 3):
        arrive(move_in.at[slot, pl.ds(0, n_panel - 1)], move_send.at[slot])
    for slot in range(2 * ITERS + 2):
        n = n_panel if slot in (1, 2, 4, 6, 8) else n_dom
        arrive(sum_in.at[slot, pl.ds(0, n - 1)], sum_send.at[slot])

    ritz_column = to_column(ritz + SHIFT)
    narrow = lax.broadcasted_iota(jnp.int32, (width, LANES), 1) == lax.broadcasted_iota(
        jnp.int32, (width, LANES), 0
    )
    ritz_ref[...] = jnp.sum(jnp.where(narrow, ritz_column, 0.0), axis=0, keepdims=True)

    def put_dirs(b, value):
        dirs_ref[:, b * LANES : (b + 1) * LANES] = value

    wait_move(f_dirs)
    assemble(f_dirs, put_dirs)
    def put_field(b, value):
        field[K, b] = value

    wait_move(f_block)
    assemble(f_block, put_field)
    scale = to_column(inverse_factor(wait_sum("dom", 2 * ITERS + 1)))
    for b in range(blocks):
        block_ref[:, b * LANES : (b + 1) * LANES] = field[K, b] * scale


def publish(block_in, dirs_in, ritz_in, block_ref, dirs_ref, ritz_ref, sems):
    block_ref[...] = block_in[...]
    dirs_ref[...] = dirs_in[...]
    ritz_ref[...] = ritz_in[:, : ritz_ref.shape[1]]


def local(n_dom, n_panel, *args):
    start, prior, degree, tiles, trows, tcols, cuts, count, btiles, brows, bcols = args[:11]
    width, ndev = start.shape
    blocks = ndev // LANES
    n_tiles, n_bound, n_cut = tiles.shape[0], btiles.shape[0], cuts.shape[0]
    rows = args[11].shape[0]
    f32, bf16, i32 = jnp.float32, jnp.bfloat16, jnp.int32
    vmem, dma = pltpu.VMEM, pltpu.SemaphoreType.DMA
    n_far, n_move, n_sum = 2 * ITERS - 1, 2 * ITERS + 3, 2 * ITERS + 2

    def smem(shape):
        return pltpu.SMEM(shape, i32)

    scratch = [
        vmem((width, ndev), f32),
        vmem((width, ndev), f32),
        vmem((1, ndev), f32),
        vmem(tiles.shape, f32),
        smem(trows.shape),
        smem(tcols.shape),
        vmem((1, n_cut), i32),
        vmem((1, 1), i32),
        vmem(btiles.shape, f32),
        smem(brows.shape),
        smem(bcols.shape),
        vmem((5, rows, rows), f32),
        dma((16,)),
        vmem((ndev, n_cut), bf16),
        vmem((n_tiles, LANES, 2 * LANES), bf16),
        vmem((n_bound, 2 * LANES, LANES), bf16),
        vmem((rows, 2 * rows), bf16),
        vmem((rows, 2 * rows), bf16),
        vmem((2, rows, 4 * rows), bf16),
        vmem((rows, 4 * rows), bf16),
        vmem((2, blocks, width, LANES), f32),
        vmem((blocks, 4 * width, 2 * LANES), bf16),
        vmem((2, blocks, width, LANES), f32),
        vmem((2, 2 * rows, (ITERS + 1) * LANES), bf16),
        vmem((2, 2 * rows, ITERS * LANES), bf16),
        vmem((n_far, n_cut // LANES, width, LANES), f32),
        (vmem((n_dom * n_cut // LANES, width, LANES), f32),) * n_far,
        vmem((n_move, n_panel, 8, LANES), f32),
        vmem((n_move, n_panel, 8, LANES), f32),
        vmem((n_sum, 2, rows), f32),
        vmem((n_sum, max(n_dom, n_panel), 2, rows), f32),
    ]
    for slots in (n_far, n_move, n_sum):
        scratch += [dma((slots,)), dma((slots,))]

    block, dirs, ritz = pl.pallas_call(
        functools.partial(kernel, ndev * n_dom),
        out_shape=(
            jax.ShapeDtypeStruct((width, ndev), f32),
            jax.ShapeDtypeStruct((width, ndev), f32),
            jax.ShapeDtypeStruct((1, LANES), f32),
        ),
        in_specs=[pl.BlockSpec(memory_space=pl.ANY)] * 16,
        out_specs=(pl.BlockSpec(memory_space=pltpu.VMEM),) * 3,
        scratch_shapes=scratch,
        compiler_params=pltpu.CompilerParams(
            collective_id=0, has_side_effects=True, vmem_limit_bytes=60 * 1024 * 1024
        ),
    )(
        start,
        prior,
        degree.reshape(1, -1),
        tiles,
        trows,
        tcols,
        cuts.reshape(1, -1),
        count.reshape(1, 1),
        btiles,
        brows,
        bcols,
        *args[11:],
    )
    block, dirs, ritz = pl.pallas_call(
        publish,
        out_shape=(
            jax.ShapeDtypeStruct((width, ndev), f32),
            jax.ShapeDtypeStruct((width, ndev), f32),
            jax.ShapeDtypeStruct((1, width), f32),
        ),
        in_specs=[pl.BlockSpec(memory_space=pltpu.VMEM)] * 2
        + [pl.BlockSpec(memory_space=pltpu.VMEM)],
        out_specs=[pl.BlockSpec(memory_space=pltpu.VMEM)] * 2
        + [pl.BlockSpec(memory_space=pltpu.VMEM)],
        scratch_shapes=[dma((2,))],
    )(block, dirs, ritz)
    return block, dirs, ritz.reshape(-1)


def solution(mesh):
    return jax.shard_map(
        functools.partial(local, mesh.shape["dom"], mesh.shape["panel"]),
        mesh=mesh,
        in_specs=(
            P("panel", "dom"),
            P("panel", "dom"),
            P("dom"),
            P("dom", None, None),
            P("dom"),
            P("dom"),
            P("dom"),
            P("dom"),
            P("dom", None, None),
            P("dom"),
            P("dom"),
            P(),
            P(),
            P(),
            P(),
            P(),
        ),
        out_specs=(P("panel", "dom"), P("panel", "dom"), P("panel")),
        check_vma=False,
    )
```

```python
import functools
import math

import jax
import jax.numpy as jnp
from jax import lax
from jax.experimental import pallas as pl
from jax.experimental.pallas import tpu as pltpu
from jax.sharding import PartitionSpec as P

ITERS = 4
MESH = pl.DeviceIdType.MESH
LANES = 128
HALF = 64
UNROLL = 16
K, Q = 0, 1
SHIFT = 2.5


def split(value):
    high = value.astype(jnp.bfloat16)
    low = (value - high.astype(jnp.float32)).astype(jnp.bfloat16)
    return high, low


def swap(value):
    return pltpu.roll(value, HALF, value.ndim - 1)


def left_half(shape):
    return lax.broadcasted_iota(jnp.int32, shape, len(shape) - 1) < HALF


def dot(left, right):
    return jnp.dot(left, right, preferred_element_type=jnp.float32)


def dot_transposed(left, right):
    return lax.dot_general(
        left, right, (((1,), (1,)), ((), ())), preferred_element_type=jnp.float32
    )


def kernel(
    nodes,
    start_hbm,
    prior_hbm,
    degree_hbm,
    tiles_hbm,
    trows_hbm,
    tcols_hbm,
    cuts_hbm,
    count_hbm,
    btiles_hbm,
    brows_hbm,
    bcols_hbm,
    xx_hbm,
    xr_hbm,
    xp_hbm,
    pr_hbm,
    pp_hbm,
    block_ref,
    dirs_ref,
    ritz_ref,
    start_ref,
    prior_ref,
    degree_ref,
    tiles_ref,
    trows,
    tcols,
    cuts_ref,
    count,
    btiles_ref,
    brows,
    bcols,
    rot_ref,
    load_sem,
    onehot,
    weights,
    bweights,
    xp_cat,
    pp_cat,
    y_cat,
    p_cat,
    field,
    stacked,
    acc,
    y_data,
    p_data,
    far_out,
    far_in,
    move_out,
    move_in,
    sum_out,
    sum_in,
    far_send,
    far_recv,
    move_send,
    move_recv,
    sum_send,
    sum_recv,
):
    dom, panel = lax.axis_index("dom"), lax.axis_index("panel")
    n_dom, n_panel = lax.axis_size("dom"), lax.axis_size("panel")
    blocks, width = field.shape[1], field.shape[2]
    n_tiles, n_bound = weights.shape[0], bweights.shape[0]
    rows = rot_ref.shape[1]
    n_cut = cuts_ref.shape[1]
    halves = n_cut // LANES
    f32, bf16 = jnp.float32, jnp.bfloat16

    side = math.isqrt(n_dom)
    dom_y, dom_x = dom // side, dom % side
    panel_z, core = panel // 2, panel % 2
    dom_steps = [(y, x) for y in range(n_dom // side) for x in range(side)][1:]
    dom_steps.sort(key=lambda s: -min(s[0], n_dom // side - s[0]) - min(s[1], side - s[1]))
    panel_steps = [(z, c) for z in range(n_panel // 2) for c in range(2)][1:]
    panel_steps.sort(key=lambda s: -min(s[0], n_panel // 2 - s[0]))
    peers = {
        "dom": [
            (dom_y + y) % (n_dom // side) * side + (dom_x + x) % side for y, x in dom_steps
        ],
        "panel": [(panel_z + z) % (n_panel // 2) * 2 + (core + c) % 2 for z, c in panel_steps],
    }

    barrier = pltpu.get_barrier_semaphore()
    for axis in ("dom", "panel"):
        for peer in peers[axis]:
            pl.semaphore_signal(barrier, inc=1, device_id={axis: peer}, device_id_type=MESH)

    loads = []

    def load(src, dst):
        copy = pltpu.make_async_copy(src, dst, load_sem.at[len(loads)])
        copy.start()
        loads.append(copy)
        return copy

    got_cuts = load(cuts_hbm, cuts_ref)
    got_count = load(count_hbm, count)
    got_start = load(start_hbm, start_ref)
    got_prior = load(prior_hbm, prior_ref)
    got_index = [
        load(trows_hbm, trows),
        load(tcols_hbm, tcols),
        load(brows_hbm, brows),
        load(bcols_hbm, bcols),
        load(degree_hbm, degree_ref),
    ]
    got_tiles = load(tiles_hbm, tiles_ref)
    got_btiles = load(btiles_hbm, btiles_ref)
    got_rot = [
        load(src, rot_ref.at[at])
        for at, src in enumerate((xx_hbm, xr_hbm, xp_hbm, pr_hbm, pp_hbm))
    ]

    def spread(axis, source, target, send, recv):
        me = dom if axis == "dom" else panel
        for peer in peers[axis]:
            pltpu.make_async_remote_copy(
                src_ref=source(peer),
                dst_ref=target(me),
                send_sem=send,
                recv_sem=recv,
                device_id={axis: peer},
                device_id_type=MESH,
            ).start()

    def arrive(like, sem):
        pltpu.make_async_copy(like, like, sem).wait()


    def set_block(kind, b, value):
        field[kind, b] = value
        high, low = split(value)
        both = jnp.concatenate([high, low], axis=0)
        at = kind * 2 * width
        stacked[b, at : at + 2 * width] = jnp.concatenate([both, both], axis=1)

    def choose(kind, j):
        at = kind * 2 * width
        chosen = jnp.zeros((2 * width, n_cut), f32)
        for b in range(blocks):
            chosen += dot(
                stacked[b, at : at + 2 * width, :LANES], onehot[b * LANES : (b + 1) * LANES]
            )
        chosen = chosen[:width] + chosen[width:]
        slot = 2 * j + kind
        for h in range(halves):
            far_out[slot, h] = chosen[:, h * LANES : (h + 1) * LANES]

    def send_far(kind, j):
        slot = 2 * j + kind
        spread(
            "dom",
            lambda q: far_out.at[slot],
            lambda q: far_in[slot].at[pl.ds(q * halves, halves)],
            far_send.at[slot],
            far_recv.at[slot],
        )
        far_in[slot][pl.ds(dom * halves, halves)] = far_out[slot]

    def collect(totals, products, row_ids):
        totals = list(totals)
        for product, row in zip(products, row_ids):
            for r in range(blocks):
                totals[r] = totals[r] + jnp.where(row == r, product, 0.0)
        return tuple(totals)

    def interior(kinds):
        wide = 2 * width * len(kinds)

        def step(i, totals):
            products, row_ids = [], []
            for u in range(min(UNROLL, n_tiles)):
                t = i * min(UNROLL, n_tiles) + u
                product = dot_transposed(stacked[tcols[t], :wide], weights[t])
                parts = [
                    product[2 * width * n : 2 * width * n + width]
                    + product[2 * width * n + width : 2 * width * (n + 1)]
                    for n in range(len(kinds))
                ]
                products.append(jnp.concatenate(parts, axis=0))
                row_ids.append(trows[t])
            return collect(totals, products, row_ids)

        zero = jnp.zeros((width * len(kinds), LANES), f32)
        totals = lax.fori_loop(0, n_tiles // min(UNROLL, n_tiles), step, (zero,) * blocks)
        for b in range(blocks):
            for n in range(len(kinds)):
                acc[n, b] = totals[b][n * width : (n + 1) * width]

    def boundary(kind, j):
        slot = 2 * j + kind
        arrive(far_in[slot].at[pl.ds(0, (n_dom - 1) * halves)], far_recv.at[slot])

        def step(i, totals):
            products, row_ids = [], []
            for u in range(min(UNROLL, n_bound)):
                t = i * min(UNROLL, n_bound) + u
                high, low = split(far_in[slot][bcols[t]])
                both = jnp.concatenate([high, low], axis=0)
                product = dot(jnp.concatenate([both, both], axis=1), bweights[t])
                products.append(product[:width] + product[width:])
                row_ids.append(brows[t])
            return collect(totals, products, row_ids)

        totals = lax.fori_loop(
            0,
            n_bound // min(UNROLL, n_bound),
            step,
            tuple(acc[kind, b] for b in range(blocks)),
        )
        return [
            (degree_ref[:, b * LANES : (b + 1) * LANES] - SHIFT) * field[kind, b] - totals[b]
            for b in range(blocks)
        ]

    left8 = left_half((8, LANES))

    def send_nodes(slot, values):
        for b in range(blocks):
            value = values(b)
            top, bottom = value[:8], value[8:]
            move_out[slot, 2 * b] = jnp.where(left8, top, swap(bottom))
            move_out[slot, 2 * b + 1] = jnp.where(left8, swap(top), bottom)
        move(slot)

    def move(slot):
        spread(
            "panel",
            lambda q: move_out.at[slot, q],
            lambda q: move_in.at[slot, q],
            move_send.at[slot],
            move_recv.at[slot],
        )
        move_in[slot, panel] = move_out[slot, panel]

    def wait_move(slot):
        arrive(move_in.at[slot, pl.ds(0, n_panel - 1)], move_recv.at[slot])

    def assemble(slot, put):
        for b in range(blocks):
            first, second = move_in[slot, 2 * b], move_in[slot, 2 * b + 1]
            top = jnp.where(left8, first, swap(second))
            bottom = jnp.where(left8, swap(first), second)
            put(b, jnp.concatenate([top, bottom], axis=0))


    def unpack(slot):
        got = move_in[slot]
        turned = swap(got)
        left = left_half(got.shape)
        top = jnp.where(left, got, turned)
        bottom = jnp.where(left, turned, got)
        return jnp.concatenate([top[:, None], bottom[:, None]], axis=1).reshape(rows, LANES)

    left_rows = left_half((rows, LANES))

    def put_operand(data, at, j, value):
        high = value.astype(bf16).astype(f32)
        lanes = slice(j * LANES, (j + 1) * LANES)
        data[at, :rows, lanes] = jnp.where(left_rows, high, value - high).astype(bf16)
        data[at, rows:, lanes] = jnp.where(left_rows, high, 0.0).astype(bf16)

    def receive(data, slot, j):
        wait_move(slot)
        put_operand(data, 0, j, unpack(slot))

    def put_matrix(ref, at, matrix):
        high, low = split(matrix)
        ref[:, at * 2 * rows : at * 2 * rows + rows] = high
        ref[:, at * 2 * rows + rows : (at + 1) * 2 * rows] = low

    def scale_matrices(k, total):
        scale = inverse_factor(total)
        ritz = total[1:2] / total[0:1]
        xr_scaled = rot_ref[1] * scale
        put_matrix(y_cat.at[k % 2], 0, rot_ref[0] * scale - xr_scaled * ritz)
        put_matrix(y_cat.at[k % 2], 1, xr_scaled)
        return scale, ritz

    def scale_direction_matrices(scale, ritz):
        pr_scaled = rot_ref[3] * scale
        put_matrix(p_cat, 0, -pr_scaled * ritz)
        put_matrix(p_cat, 1, pr_scaled)

    def new_y(k, first, count, base=None):
        return rotate(y_cat.at[k % 2], xp_cat, k, first, count, base)

    def new_p(k, first, count):
        return rotate(p_cat, pp_cat, k, first, count)

    def put_y(k, first, values):
        for n, value in enumerate(values):
            put_operand(y_data, (k + 1) % 2, first + n, value)

    def put_p(k, first, values):
        for n, value in enumerate(values):
            put_operand(p_data, (k + 1) % 2, first + n, value)

    def from_directions(from_cat, k, first, count):
        return dot(from_cat[...], p_data[k % 2, :, first * LANES : (first + count) * LANES])

    def rotate(matrices, from_cat, k, first, count, base=None):
        now = k % 2
        lo, hi = first * LANES, (first + count) * LANES
        total = from_directions(from_cat, k, first, count) if base is None else base
        total += dot(matrices[:, : 2 * rows], y_data[now, :, lo:hi])
        total += dot(matrices[:, 2 * rows :], y_data[now, :, lo + LANES : hi + LANES])
        values = []
        for n in range(count):
            part = total[:, n * LANES : (n + 1) * LANES]
            values.append(part + swap(part))
        return values

    def pack(slot, value):
        value4 = value.reshape(n_panel, 2, 8, LANES)
        move_out[slot] = jnp.where(
            left_half((n_panel, 8, LANES)), value4[:, 0], value4[:, 1]
        )


    def send_sum(axis, slot, value):
        sum_out[slot] = value
        spread(
            axis,
            lambda q: sum_out.at[slot],
            lambda q: sum_in.at[slot, q],
            sum_send.at[slot],
            sum_recv.at[slot],
        )
        sum_in[slot, dom if axis == "dom" else panel] = value

    def wait_sum(axis, slot):
        n = n_dom if axis == "dom" else n_panel
        arrive(sum_in.at[slot, pl.ds(0, n - 1)], sum_recv.at[slot])
        return jnp.sum(sum_in[slot, :n], axis=0)

    own = lax.broadcasted_iota(jnp.int32, (width, rows), 1) == (
        lax.broadcasted_iota(jnp.int32, (width, rows), 0) + panel * width
    )

    def to_row(partial):
        column = jnp.sum(partial, axis=1, keepdims=True)
        return jnp.sum(jnp.where(own, column, 0.0), axis=0, keepdims=True)

    def to_column(row):
        return jnp.sum(jnp.where(own, row, 0.0), axis=1, keepdims=True)

    pick_row = lax.broadcasted_iota(jnp.int32, (width, 2 * LANES), 0)
    pick_lane = lax.broadcasted_iota(jnp.int32, (width, 2 * LANES), 1) // HALF % 2
    pick = (pick_row == pick_lane).astype(f32).astype(bf16)

    def node_sums(first, second):
        product = first * jnp.where(left_rows, first, second)
        high, low = split(product)
        return dot_transposed(pick, jnp.concatenate([high, low], axis=1))[:2]

    def inverse_factor(total):
        return 1.0 / jnp.sqrt(total[0:1] / nodes + 1e-06)


    got_cuts.wait()
    got_count.wait()
    cut = jnp.where(
        lax.broadcasted_iota(jnp.int32, (1, n_cut), 1) < count[...], cuts_ref[...], -1
    )
    for b in range(blocks):
        row = lax.broadcasted_iota(jnp.int32, (LANES, n_cut), 0) + b * LANES
        onehot[b * LANES : (b + 1) * LANES] = (row == cut).astype(f32).astype(bf16)
    got_start.wait()
    for b in range(blocks):
        set_block(K, b, start_ref[:, b * LANES : (b + 1) * LANES])
    got_prior.wait()
    for b in range(blocks):
        set_block(Q, b, prior_ref[:, b * LANES : (b + 1) * LANES])

    choose(K, 0)
    choose(Q, 0)
    pl.semaphore_wait(barrier, n_dom + n_panel - 2)

    def split_turned(source, target):
        def step(t, _):
            high, low = split(source[t].T)
            target[t] = jnp.concatenate([high, low], axis=0)
            return 0

        lax.fori_loop(0, source.shape[0], step, 0)

    def split_tiles(source, target):
        def step(t, _):
            high, low = split(source[t])
            target[t] = jnp.concatenate([high, low], axis=1)
            return 0

        lax.fori_loop(0, source.shape[0], step, 0)

    def advance(kind, j):
        images = boundary(kind, j)
        if j > 0:
            send_nodes(2 * (j + 1) + kind, lambda b: images[b])
        if kind == K and j == 0:
            cross = jnp.zeros((width, LANES), f32)
            for b in range(blocks):
                cross += field[K, b] * images[b]
            send_sum("dom", 0, jnp.concatenate([square_row, to_row(cross)], axis=0))
        for b in range(blocks):
            set_block(kind, b, images[b])
        if j + 1 < ITERS - kind:
            choose(kind, j + 1)
            send_far(kind, j + 1)
        if j == 0:
            send_nodes(2 * (j + 1) + kind, lambda b: images[b])

    f_block, f_dirs = 2 * ITERS + 1, 2 * ITERS + 2

    send_far(K, 0)
    got_tiles.wait()
    split_tiles(tiles_ref, weights)
    send_far(Q, 0)
    got_btiles.wait()
    split_turned(btiles_ref, bweights)
    for copy in got_index:
        copy.wait()
    interior((K, Q))
    send_nodes(0, lambda b: field[K, b])
    send_nodes(1, lambda b: field[Q, b])
    square = jnp.zeros((width, LANES), f32)
    for b in range(blocks):
        square += field[K, b] * field[K, b]
    square_row = to_row(square)
    advance(K, 0)
    advance(Q, 0)
    interior((K, Q))
    send_sum("panel", 1, wait_sum("dom", 0))
    advance(K, 1)
    for copy in got_rot:
        copy.wait()
    put_matrix(xp_cat, 0, rot_ref[2])
    put_matrix(pp_cat, 0, rot_ref[4])
    receive(y_data, 0, 0)
    receive(p_data, 1, 0)
    receive(y_data, 2, 1)
    receive(p_data, 3, 1)

    base = from_directions(xp_cat, 0, 0, 2)
    scale, ritz = scale_matrices(0, wait_sum("panel", 1))
    base += dot(y_cat[0, :, : 2 * rows], y_data[0, :, : 2 * LANES])
    near = base[:, :LANES] + dot(y_cat[0, :, 2 * rows :], y_data[0, :, LANES : 2 * LANES])
    advance(Q, 1)
    receive(y_data, 4, 2)
    next_ = base[:, LANES:] + dot(y_cat[0, :, 2 * rows :], y_data[0, :, 2 * LANES : 3 * LANES])
    now = [near + swap(near), next_ + swap(next_)]
    send_sum("panel", 2, node_sums(now[0], now[1]))
    put_y(0, 0, now)
    interior((K, Q))
    advance(K, 2)
    scale_direction_matrices(scale, ritz)
    put_p(0, 0, new_p(0, 0, 2))
    send_sum("dom", 3, wait_sum("panel", 2))
    advance(Q, 2)
    interior((K,))
    receive(p_data, 5, 2)
    receive(y_data, 6, 3)
    put_y(0, 2, new_y(0, 2, 1))
    put_p(0, 2, new_p(0, 2, 1))

    base = from_directions(xp_cat, 1, 0, 2)
    scale, ritz = scale_matrices(1, wait_sum("dom", 3))
    now = new_y(1, 0, 2, base)
    send_sum("panel", 4, node_sums(now[0], now[1]))
    put_y(1, 0, now)
    advance(K, 3)
    scale_direction_matrices(scale, ritz)
    put_p(1, 0, new_p(1, 0, 2))
    send_sum("dom", 5, wait_sum("panel", 4))
    receive(p_data, 7, 3)
    receive(y_data, 8, 4)
    put_y(0, 3, new_y(0, 3, 1))
    put_y(1, 2, new_y(1, 2, 1))

    base = from_directions(xp_cat, 2, 0, 2)
    scale, ritz = scale_matrices(2, wait_sum("dom", 5))
    now = new_y(2, 0, 2, base)
    send_sum("panel", 6, node_sums(now[0], now[1]))
    put_y(2, 0, now)
    scale_direction_matrices(scale, ritz)
    put_p(2, 0, new_p(2, 0, 1))
    send_sum("dom", 7, wait_sum("panel", 6))

    base = from_directions(xp_cat, 3, 0, 1)
    scale, ritz = scale_matrices(3, wait_sum("dom", 7))
    now = new_y(3, 0, 1, base)[0]
    send_sum("panel", 8, node_sums(now, now))
    pack(f_block, now)
    move(f_block)
    scale_direction_matrices(scale, ritz)
    pack(f_dirs, new_p(3, 0, 1)[0])
    move(f_dirs)
    send_sum("dom", 9, wait_sum("panel", 8))

    for slot in range(2 * ITERS - 1):
        arrive(far_in[slot].at[pl.ds(0, (n_dom - 1) * halves)], far_send.at[slot])
    for slot in range(2 * ITERS + 3):
        arrive(move_in.at[slot, pl.ds(0, n_panel - 1)], move_send.at[slot])
    for slot in range(2 * ITERS + 2):
        n = n_panel if slot in (1, 2, 4, 6, 8) else n_dom
        arrive(sum_in.at[slot, pl.ds(0, n - 1)], sum_send.at[slot])

    ritz_column = to_column(ritz + SHIFT)
    narrow = lax.broadcasted_iota(jnp.int32, (width, LANES), 1) == lax.broadcasted_iota(
        jnp.int32, (width, LANES), 0
    )
    ritz_ref[...] = jnp.sum(jnp.where(narrow, ritz_column, 0.0), axis=0, keepdims=True)

    def put_dirs(b, value):
        dirs_ref[:, b * LANES : (b + 1) * LANES] = value

    wait_move(f_dirs)
    assemble(f_dirs, put_dirs)
    def put_field(b, value):
        field[K, b] = value

    wait_move(f_block)
    assemble(f_block, put_field)
    scale = to_column(inverse_factor(wait_sum("dom", 2 * ITERS + 1)))
    for b in range(blocks):
        block_ref[:, b * LANES : (b + 1) * LANES] = field[K, b] * scale


def publish(block_in, dirs_in, ritz_in, block_ref, dirs_ref, ritz_ref, sems):
    block_ref[...] = block_in[...]
    dirs_ref[...] = dirs_in[...]
    ritz_ref[...] = ritz_in[:, : ritz_ref.shape[1]]


def local(n_dom, n_panel, *args):
    start, prior, degree, tiles, trows, tcols, cuts, count, btiles, brows, bcols = args[:11]
    width, ndev = start.shape
    blocks = ndev // LANES
    n_tiles, n_bound, n_cut = tiles.shape[0], btiles.shape[0], cuts.shape[0]
    rows = args[11].shape[0]
    f32, bf16, i32 = jnp.float32, jnp.bfloat16, jnp.int32
    vmem, dma = pltpu.VMEM, pltpu.SemaphoreType.DMA
    n_far, n_move, n_sum = 2 * ITERS - 1, 2 * ITERS + 3, 2 * ITERS + 2

    def smem(shape):
        return pltpu.SMEM(shape, i32)

    scratch = [
        vmem((width, ndev), f32),
        vmem((width, ndev), f32),
        vmem((1, ndev), f32),
        vmem(tiles.shape, f32),
        smem(trows.shape),
        smem(tcols.shape),
        vmem((1, n_cut), i32),
        vmem((1, 1), i32),
        vmem(btiles.shape, f32),
        smem(brows.shape),
        smem(bcols.shape),
        vmem((5, rows, rows), f32),
        dma((16,)),
        vmem((ndev, n_cut), bf16),
        vmem((n_tiles, LANES, 2 * LANES), bf16),
        vmem((n_bound, 2 * LANES, LANES), bf16),
        vmem((rows, 2 * rows), bf16),
        vmem((rows, 2 * rows), bf16),
        vmem((2, rows, 4 * rows), bf16),
        vmem((rows, 4 * rows), bf16),
        vmem((2, blocks, width, LANES), f32),
        vmem((blocks, 4 * width, 2 * LANES), bf16),
        vmem((2, blocks, width, LANES), f32),
        vmem((2, 2 * rows, (ITERS + 1) * LANES), bf16),
        vmem((2, 2 * rows, ITERS * LANES), bf16),
        vmem((n_far, n_cut // LANES, width, LANES), f32),
        (vmem((n_dom * n_cut // LANES, width, LANES), f32),) * n_far,
        vmem((n_move, n_panel, 8, LANES), f32),
        vmem((n_move, n_panel, 8, LANES), f32),
        vmem((n_sum, 2, rows), f32),
        vmem((n_sum, max(n_dom, n_panel), 2, rows), f32),
    ]
    for slots in (n_far, n_move, n_sum):
        scratch += [dma((slots,)), dma((slots,))]

    block, dirs, ritz = pl.pallas_call(
        functools.partial(kernel, ndev * n_dom),
        out_shape=(
            jax.ShapeDtypeStruct((width, ndev), f32),
            jax.ShapeDtypeStruct((width, ndev), f32),
            jax.ShapeDtypeStruct((1, LANES), f32),
        ),
        in_specs=[pl.BlockSpec(memory_space=pl.ANY)] * 16,
        out_specs=(pl.BlockSpec(memory_space=pltpu.VMEM),) * 3,
        scratch_shapes=scratch,
        compiler_params=pltpu.CompilerParams(
            collective_id=0, has_side_effects=True, vmem_limit_bytes=60 * 1024 * 1024
        ),
    )(
        start,
        prior,
        degree.reshape(1, -1),
        tiles,
        trows,
        tcols,
        cuts.reshape(1, -1),
        count.reshape(1, 1),
        btiles,
        brows,
        bcols,
        *args[11:],
    )
    block, dirs, ritz = pl.pallas_call(
        publish,
        out_shape=(
            jax.ShapeDtypeStruct((width, ndev), f32),
            jax.ShapeDtypeStruct((width, ndev), f32),
            jax.ShapeDtypeStruct((1, width), f32),
        ),
        in_specs=[pl.BlockSpec(memory_space=pltpu.VMEM)] * 2
        + [pl.BlockSpec(memory_space=pltpu.VMEM)],
        out_specs=[pl.BlockSpec(memory_space=pltpu.VMEM)] * 2
        + [pl.BlockSpec(memory_space=pltpu.VMEM)],
        scratch_shapes=[dma((2,))],
    )(block, dirs, ritz)
    return block, dirs, ritz.reshape(-1)


def solution(mesh):
    return jax.shard_map(
        functools.partial(local, mesh.shape["dom"], mesh.shape["panel"]),
        mesh=mesh,
        in_specs=(
            P("panel", "dom"),
            P("panel", "dom"),
            P("dom"),
            P("dom", None, None),
            P("dom"),
            P("dom"),
            P("dom"),
            P("dom"),
            P("dom", None, None),
            P("dom"),
            P("dom"),
            P(),
            P(),
            P(),
            P(),
            P(),
        ),
        out_specs=(P("panel", "dom"), P("panel", "dom"), P("panel")),
        check_vma=False,
    )
```
